32 devices in a mesh: rep: 2 (over x), asset: 8 (over z, y), sample: 2 (over core).
Axes of the slice: x: 2, y: 2, z: 4, core: 2. Of those that a mesh axis runs over, the one named last changes fastest.
Arguments:
- samples: float32 [8, 1024, 32768], P(('rep', 'sample'), None, 'asset'), parts along dimension 0, may hold values from -40 to 40, as said below
- start_panel: float32 [32768, 128], P('asset'), may hold values from -6 to 6
Outputs:
- local_panels: float32 [8, 32768, 128], P(('rep', 'sample'), 'asset'), parts along dimension 0
- subspace: float32 [65536, 128], P(('rep', 'asset')), parts along dimension 0
The draws below stay inside these ranges and needn't reach their ends.
There are 2 independent parts, one for each index of `rep`. The reference program is written for one: setup_inputs(seed, part) draws one part's arguments, and reference() takes and returns one part's arrays. A program takes and returns all parts, laid end to end along the dimension named above; an argument that names none is the same for every part. Nothing has to cross between parts.
Inputs may be any that keep to these rules, and one draw needn't show every extreme that they name: `samples`: returns of each asset with an asset-specific volatility.
All inputs are finite; a program needn't handle non-finite values.
Results may differ from the reference program's by a relative error of at most 0.0003.
Values sent between devices are 32-bit elements; how exact they have to be, the bound alone decides.
No kernel may reach another device: no remote copies, remote signals or barrier semaphores. Data moves between devices by JAX's collectives and lax.ppermute only.
A program may use at most 192 MiB of HBM per device.

```python
import jax
import jax.numpy as jnp
from jax import lax

ASSETS = 32768
K = 128
SAMPLES = 1024
LOCAL_ITERS = 2
FINAL_ITERS = 4
GROUPS = 4


def draw_samples(key, part):
    key = jax.random.fold_in(key, 3)
    scale_key, value_key = jax.random.split(key, 2)
    scales = jnp.exp(jax.random.uniform(scale_key, (1, 1, ASSETS), jnp.float32, jnp.log(0.5), jnp.log(5.0)))
    values = jnp.clip(jax.random.normal(value_key, (GROUPS, SAMPLES, ASSETS), jnp.float32), -6.0, 6.0)
    return values * scales


def levels(key, dims, cuts, smallest, high):
    factor_of, own = 1.0, jax.random.fold_in(key, 6)
    for dim, shards_of in cuts:
        steps = jnp.exp(jax.random.uniform(jax.random.fold_in(own, dim), (shards_of,), jnp.float32, smallest / len(cuts), high / len(cuts)))
        factor_of = factor_of * jnp.repeat(steps, dims[dim] // shards_of).reshape([-1 if axis == dim else 1 for axis in range(len(dims))])
    return factor_of


def noise(stream_key, extent, deviation, bound, cuts=(), dtype=jnp.bfloat16):
    loudness = levels(stream_key, extent, cuts, -0.22, 0.18) if cuts else 1.0
    array = jax.random.normal(stream_key, extent, jnp.float32) * deviation * loudness
    return jnp.minimum(jnp.maximum(array, -bound), bound).astype(dtype)


def setup_inputs(seed: int = 0, part: int = 0) -> dict:
    splits = jax.random.split(jax.random.key(seed), 3)
    own_keys = jax.random.split(jax.random.fold_in(splits[2], part), 3)
    samples = draw_samples(jax.random.fold_in(jax.random.fold_in(splits[2], part), 71), part)
    start_panel = noise(splits[1], (ASSETS, K), 1.0, 6.0, ((0, 8),), jnp.float32)
    return dict(samples=samples, start_panel=start_panel)


HIGH = lax.Precision.HIGHEST

def orthonormal(expanded_panel, width_all):
    gram_matrix = jnp.einsum('...ak,...al->...kl', expanded_panel, expanded_panel, precision=HIGH) / width_all
    cholesky_factor = jnp.linalg.cholesky(gram_matrix)
    solved = jax.scipy.linalg.solve_triangular(cholesky_factor, jnp.swapaxes(expanded_panel, -1, -2), lower=True)
    return jnp.swapaxes(solved, -1, -2)

def one_group(group_samples, start_panel):
    panels = start_panel
    for iteration in range(LOCAL_ITERS):
        scores = jnp.dot(group_samples, panels, precision=HIGH)
        expanded = jnp.dot(group_samples.T, scores, precision=HIGH)
        panels = orthonormal(expanded, ASSETS)
    return panels

def reference(samples, start_panel):
    local_panels = lax.map(lambda group_samples: one_group(group_samples, start_panel), samples)
    subspace = start_panel
    for iteration in range(FINAL_ITERS):
        correlations = jnp.einsum('gak,al->gkl', local_panels, subspace, precision=HIGH)
        averaged = jnp.einsum('gak,gkl->al', local_panels, correlations, precision=HIGH) / GROUPS
        subspace = orthonormal(averaged, ASSETS)
    return (local_panels, subspace)
```

```python
import functools

import jax
import jax.numpy as jnp
from jax import lax
from jax.experimental import pallas as pl
from jax.experimental.pallas import tpu as pltpu
from jax.sharding import PartitionSpec as P

LOCAL_ITERS = 2
FINAL_ITERS = 4


HIGH = lax.Precision.HIGHEST
THREE = lax.Precision.HIGH
TILE = 8
PANEL = 4


def dot_exact(left, right, dims):
    return lax.dot_general(
        left, right, (dims, ((), ())), precision=HIGH, preferred_element_type=jnp.float32
    )


def inverse_factors(matrices):
    size = matrices[0].shape[0]
    blocks = size // TILE
    full = (TILE, size)
    sublane = lax.broadcasted_iota(jnp.int32, full, 0)
    lane = lax.broadcasted_iota(jnp.int32, full, 1)
    left, right = [], []
    for matrix in matrices:
        symmetric = 0.5 * (matrix + matrix.T)
        left.append([symmetric[TILE * i : TILE * (i + 1)] for i in range(blocks)])
        right.append(
            [jnp.where(lane == sublane + TILE * i, 1.0, 0.0) for i in range(blocks)]
        )
    along = lambda block, row: jnp.broadcast_to(block[row : row + 1], full)
    across = lambda block, column: jnp.broadcast_to(block[:, column : column + 1], full)
    for panel in range(0, blocks, PANEL):
        last = panel + PANEL
        for j in range(panel, last):
            for a, b in zip(left, right):
                columns = [across(a[j], TILE * j + k) for k in range(TILE)]
                d = [[along(columns[k], i) for k in range(i + 1)] for i in range(TILE)]
                scale = []
                for k in range(TILE):
                    scale.append(lax.rsqrt(d[k][k]))
                    for i in range(k + 1, TILE):
                        d[i][k] = d[i][k] * scale[k]
                    for i in range(k + 1, TILE):
                        for m in range(k + 1, i + 1):
                            d[i][m] = d[i][m] - d[i][k] * d[m][k]

                def substitute(parts):
                    for k in range(TILE):
                        for m in range(k):
                            parts[k] = parts[k] - d[k][m] * parts[m]
                        parts[k] = parts[k] * scale[k]
                    return parts

                rows_a = substitute([along(a[j], k) for k in range(TILE)])
                rows_b = substitute([along(b[j], k) for k in range(TILE)])
                for i in range(j + 1, last):
                    weights = substitute([across(a[i], TILE * j + k) for k in range(TILE)])
                    for k in range(TILE):
                        a[i] = a[i] - weights[k] * rows_a[k]
                        b[i] = b[i] - weights[k] * rows_b[k]

                def gather(rows):
                    block = rows[0]
                    for k in range(1, TILE):
                        block = jnp.where(sublane == k, rows[k], block)
                    return block

                a[j], b[j] = gather(rows_a), gather(rows_b)
        if last < blocks:
            for a, b in zip(left, right):
                top_a = jnp.concatenate(a[panel:last], axis=0)
                top_b = jnp.concatenate(b[panel:last], axis=0)
                change = dot_exact(
                    top_a[:, TILE * last :],
                    jnp.concatenate([top_a, top_b], axis=1),
                    ((0,), (0,)),
                )
                for i in range(last, blocks):
                    rows = change[TILE * (i - last) : TILE * (i - last + 1)]
                    a[i] = a[i] - rows[:, :size]
                    b[i] = b[i] - rows[:, size:]
    return [jnp.concatenate(b, axis=0) for b in right]


def normal_kernel(width_all, first_ref, second_ref, out_ref):
    count = first_ref.shape[0]
    grams = [
        dot_exact(first_ref[g], second_ref[g], ((0,), (0,))) * (1.0 / width_all)
        for g in range(count)
    ]
    for g, inverse in enumerate(inverse_factors(grams)):
        out_ref[g] = dot_exact(second_ref[g], inverse, ((1,), (1,)))


def final_kernel(width_all, gram_ref, start_ref, inverse_ref, out_ref, matrix, block):
    count, _, size = inverse_ref.shape
    at = lambda g: slice(g * size, (g + 1) * size)
    inverses = inverse_factors(
        [gram_ref[at(g), at(g)] * (1.0 / width_all) for g in range(count)]
    )
    for g in range(count):
        inverse_ref[g] = inverses[g]
        block[at(g), :] = dot_exact(inverses[g], start_ref[at(g), :], ((1,), (0,)))
        row = dot_exact(inverses[g], gram_ref[at(g), :], ((1,), (0,)))
        for h in range(count):
            matrix[at(g), at(h)] = dot_exact(row[:, at(h)], inverses[h], ((1,), (1,)))

    def step(_, carry):
        held = block[...] * (1.0 / count)
        product = dot_exact(matrix[...], held, ((1,), (0,)))
        small = dot_exact(held, product, ((0,), (0,))) * (1.0 / width_all)
        (inverse,) = inverse_factors([small])
        out_ref[...] = dot_exact(held, inverse, ((1,), (1,)))
        block[...] = dot_exact(product, inverse, ((1,), (1,)))
        return carry

    lax.fori_loop(0, FINAL_ITERS, step, 0)
    held = [
        dot_exact(inverses[g], out_ref[at(g), :], ((0,), (0,))) for g in range(count)
    ]
    for g in range(count):
        out_ref[at(g), :] = held[g]


def normalise(first, second, width_all):
    return pl.pallas_call(
        functools.partial(normal_kernel, width_all),
        out_shape=jax.ShapeDtypeStruct(second.shape, jnp.float32),
        compiler_params=pltpu.CompilerParams(vmem_limit_bytes=32 * 1024 * 1024),
    )(first, second)


def final_iterations(gram, start, width_all, groups_all):
    size = start.shape[-1]
    return pl.pallas_call(
        functools.partial(final_kernel, width_all),
        out_shape=(
            jax.ShapeDtypeStruct((groups_all, size, size), jnp.float32),
            jax.ShapeDtypeStruct((groups_all * size, size), jnp.float32),
        ),
        scratch_shapes=[
            pltpu.VMEM((groups_all * size, groups_all * size), jnp.float32),
            pltpu.VMEM((groups_all * size, size), jnp.float32),
        ],
        compiler_params=pltpu.CompilerParams(vmem_limit_bytes=32 * 1024 * 1024),
    )(gram, start)


def bit_orders(bits):
    return [list(range(bits)), list(range(1, bits)) + [0]]


def total_over_assets(value):
    count, cores = lax.axis_size("asset"), lax.axis_size("sample")
    bits = count.bit_length() - 1
    orders = bit_orders(bits)
    place, core = lax.axis_index("asset"), lax.axis_index("sample")

    def exchange(held, stage):
        pairs = [
            (a * cores + c, (a ^ (1 << orders[c % 2][stage])) * cores + c)
            for a in range(count)
            for c in range(cores)
        ]
        return lax.ppermute(held, ("asset", "sample"), pairs)

    def my_bit(stage):
        bit = jnp.where(core % 2 == 0, orders[0][stage], orders[1][stage])
        return (place >> bit) & 1

    shape = value.shape
    held = value.reshape((-1, shape[-1]))
    for stage in range(bits):
        halves = held.reshape((2, -1, shape[-1]))
        mine = my_bit(stage)
        sent = lax.dynamic_index_in_dim(halves, 1 - mine, 0, keepdims=False)
        kept = lax.dynamic_index_in_dim(halves, mine, 0, keepdims=False)
        held = kept + exchange(sent, stage)
    for stage in reversed(range(bits)):
        other = exchange(held, stage)
        mine = my_bit(stage)
        held = jnp.where(
            mine == 0,
            jnp.concatenate([held, other], axis=0),
            jnp.concatenate([other, held], axis=0),
        )
    return held.reshape(shape)


def total_direct(value):
    count = lax.axis_size("asset")
    place = lax.axis_index("asset")
    shape = value.shape
    parts = value.reshape((count, -1, shape[-1]))
    part = lambda index: lax.dynamic_index_in_dim(parts, index % count, 0, keepdims=False)
    ring = lambda held, d: lax.ppermute(
        held, "asset", [(a, (a + d) % count) for a in range(count)]
    )
    total = part(place)
    for received in [ring(part(place + d), d) for d in range(1, count)]:
        total = total + received
    arrived = [total] + [ring(total, d) for d in range(1, count)]
    turned = jnp.stack(arrived[::-1] + arrived[::-1], axis=0)
    whole = lax.dynamic_slice_in_dim(turned, count - 1 - place, count, axis=0)
    return whole.reshape(shape)


def shards(samples, start_panel):
    count_local = samples.shape[0]
    rows, size = start_panel.shape
    width_all = rows * lax.axis_size("asset")
    cores = lax.axis_size("sample")
    groups_all = count_local * cores
    core = lax.axis_index("sample")
    scores = total_over_assets(
        jnp.einsum("gsa,ak->gsk", samples, start_panel, precision=THREE)
    )
    first_scores = scores
    for iteration in range(LOCAL_ITERS - 1):
        expanded = jnp.einsum("gsa,gsk->gak", samples, scores, precision=THREE)
        following = total_direct(
            jnp.einsum("gsa,gak->gsk", samples, expanded, precision=THREE)
        )
        scores = normalise(scores, following, width_all)
    expanded = jnp.einsum("gsa,gsk->gak", samples, scores, precision=THREE)
    start = jnp.einsum("gsk,gsl->gkl", scores, first_scores, precision=HIGH)

    gathered = lax.all_gather(expanded, "sample", axis=0, tiled=True)
    start = lax.all_gather(start, "sample", axis=0, tiled=True)
    part = rows // cores
    half = lax.dynamic_slice_in_dim(gathered, core * part, part, axis=1)
    flat = jnp.swapaxes(half, 0, 1).reshape((part, groups_all * size))
    partial_gram = jnp.einsum("ai,aj->ij", flat, flat, precision=HIGH)
    pairs = [(c, (c + 1) % cores) for c in range(cores)]
    shared = partial_gram
    passing = partial_gram
    for _ in range(cores - 1):
        passing = lax.ppermute(passing, "sample", pairs)
        shared = shared + passing
    gram = total_direct(shared)
    inverses, weights = final_iterations(
        gram, start.reshape((groups_all * size, size)), width_all, groups_all
    )
    own = lax.dynamic_slice_in_dim(inverses, core * count_local, count_local, axis=0)
    panels = jnp.einsum("gak,glk->gal", expanded, own, precision=HIGH)
    subspace = jnp.einsum(
        "gak,gkl->al", gathered, weights.reshape((groups_all, size, size)), precision=HIGH
    )
    return (panels, subspace)


def solution(mesh):
    placed = (P(("rep", "sample"), None, "asset"), P("asset", None))
    return jax.shard_map(
        shards,
        mesh=mesh,
        in_specs=placed,
        out_specs=(P(("rep", "sample"), "asset", None), P(("rep", "asset"), None)),
        check_vma=False,
    )
```

```python
import functools

import jax
import jax.numpy as jnp
from jax import lax
from jax.experimental import pallas as pl
from jax.experimental.pallas import tpu as pltpu
from jax.sharding import PartitionSpec as P

LOCAL_ITERS = 2
FINAL_ITERS = 4


HIGH = lax.Precision.HIGHEST
TILE = 8
PANEL = 4
WIDTH = 512
PART = 256
ROWS = 1024
MEGA = 1024 * 1024


def dot_exact(left, right, dims):
    return lax.dot_general(
        left, right, (dims, ((), ())), precision=HIGH, preferred_element_type=jnp.float32
    )


def inverse_factors(matrices):
    size = matrices[0].shape[0]
    blocks = size // TILE
    full = (TILE, size)
    sublane = lax.broadcasted_iota(jnp.int32, full, 0)
    lane = lax.broadcasted_iota(jnp.int32, full, 1)
    left, right = [], []
    for matrix in matrices:
        symmetric = 0.5 * (matrix + matrix.T)
        left.append([symmetric[TILE * i : TILE * (i + 1)] for i in range(blocks)])
        right.append(
            [jnp.where(lane == sublane + TILE * i, 1.0, 0.0) for i in range(blocks)]
        )
    along = lambda block, row: jnp.broadcast_to(block[row : row + 1], full)
    across = lambda block, column: jnp.broadcast_to(block[:, column : column + 1], full)
    for panel in range(0, blocks, PANEL):
        last = panel + PANEL
        for j in range(panel, last):
            for a, b in zip(left, right):
                columns = [across(a[j], TILE * j + k) for k in range(TILE)]
                d = [[along(columns[k], i) for k in range(i + 1)] for i in range(TILE)]
                scale = []
                for k in range(TILE):
                    scale.append(lax.rsqrt(d[k][k]))
                    for i in range(k + 1, TILE):
                        d[i][k] = d[i][k] * scale[k]
                    for i in range(k + 1, TILE):
                        for m in range(k + 1, i + 1):
                            d[i][m] = d[i][m] - d[i][k] * d[m][k]

                def substitute(parts):
                    for k in range(TILE):
                        for m in range(k):
                            parts[k] = parts[k] - d[k][m] * parts[m]
                        parts[k] = parts[k] * scale[k]
                    return parts

                rows_a = substitute([along(a[j], k) for k in range(TILE)])
                rows_b = substitute([along(b[j], k) for k in range(TILE)])
                for i in range(j + 1, last):
                    weights = substitute([across(a[i], TILE * j + k) for k in range(TILE)])
                    for k in range(TILE):
                        a[i] = a[i] - weights[k] * rows_a[k]
                        b[i] = b[i] - weights[k] * rows_b[k]

                def gather(rows):
                    block = rows[0]
                    for k in range(1, TILE):
                        block = jnp.where(sublane == k, rows[k], block)
                    return block

                a[j], b[j] = gather(rows_a), gather(rows_b)
        if last < blocks:
            for a, b in zip(left, right):
                top_a = jnp.concatenate(a[panel:last], axis=0)
                top_b = jnp.concatenate(b[panel:last], axis=0)
                change = dot_exact(
                    top_a[:, TILE * last :],
                    jnp.concatenate([top_a, top_b], axis=1),
                    ((0,), (0,)),
                )
                for i in range(last, blocks):
                    rows = change[TILE * (i - last) : TILE * (i - last + 1)]
                    a[i] = a[i] - rows[:, :size]
                    b[i] = b[i] - rows[:, size:]
    return [jnp.concatenate(b, axis=0) for b in right]


def split(value):
    high = value.astype(jnp.bfloat16)
    return high, (value - high.astype(jnp.float32)).astype(jnp.bfloat16)


def dot_short(left, right, dims=((1,), (0,))):
    return lax.dot_general(left, right, (dims, ((), ())), preferred_element_type=jnp.float32)


def call(body, grid, in_specs, out_specs, out_shape, scratch, flops, read):
    return pl.pallas_call(
        body,
        grid=grid,
        in_specs=in_specs,
        out_specs=out_specs,
        out_shape=out_shape,
        scratch_shapes=scratch,
        compiler_params=pltpu.CompilerParams(vmem_limit_bytes=40 * MEGA),
        cost_estimate=pl.CostEstimate(flops=flops, bytes_accessed=read, transcendentals=0),
    )


def project_kernel(x_ref, panel_ref, out_ref, total):
    step = pl.program_id(0)
    size = panel_ref.shape[1]

    @pl.when(step == 0)
    def _():
        total[...] = jnp.zeros_like(total)

    high, low = split(x_ref[0])
    pair = jnp.concatenate(split(panel_ref[...]), axis=1)
    total[...] += dot_short(high, pair) + dot_short(low, pair)

    @pl.when(step == pl.num_programs(0) - 1)
    def _():
        out_ref[...] = (total[:, :size] + total[:, size:]).T


def project(samples, group, panel):
    _, length, rows = samples.shape
    size = panel.shape[1]
    width = min(WIDTH, rows)
    return call(
        project_kernel,
        (rows // width,),
        [
            pl.BlockSpec((1, length, width), lambda i: (group, 0, i)),
            pl.BlockSpec((width, size), lambda i: (i, 0)),
        ],
        pl.BlockSpec((size, length), lambda i: (0, 0)),
        jax.ShapeDtypeStruct((size, length), jnp.float32),
        [pltpu.VMEM((length, 2 * size), jnp.float32)],
        8 * length * rows * size,
        4 * length * rows,
    )(samples, panel)


def expand_part(pair, high, low):
    size = pair.shape[0] // 2
    both = dot_short(pair, high)
    return (both[:size] + both[size:]) + dot_short(pair[:size], low)


def apply_kernel(x_ref, scores_ref, out_ref, pair, total):
    step = pl.program_id(0)
    size = scores_ref.shape[0]

    @pl.when(step == 0)
    def _():
        pair[...] = jnp.concatenate(split(scores_ref[...]), axis=0)
        total[...] = jnp.zeros_like(total)

    width = x_ref.shape[2]
    part = min(PART, width)
    for at in range(0, width, part):
        high, low = split(x_ref[0, :, at : at + part])
        expanded = split(expand_part(pair[...], high, low))
        both = jnp.concatenate(expanded, axis=0)
        last = ((1,), (1,))
        total[...] += dot_short(high, both, last) + dot_short(low, both, last)

    @pl.when(step == pl.num_programs(0) - 1)
    def _():
        out_ref[...] = total[:, :size] + total[:, size:]


def apply(samples, group, scores):
    _, length, rows = samples.shape
    size = scores.shape[0]
    width = min(WIDTH, rows)
    return call(
        apply_kernel,
        (rows // width,),
        [
            pl.BlockSpec((1, length, width), lambda i: (group, 0, i)),
            pl.BlockSpec((size, length), lambda i: (0, 0)),
        ],
        pl.BlockSpec((length, size), lambda i: (0, 0)),
        jax.ShapeDtypeStruct((length, size), jnp.float32),
        [
            pltpu.VMEM((2 * size, length), jnp.bfloat16),
            pltpu.VMEM((length, 2 * size), jnp.float32),
        ],
        16 * length * rows * size,
        4 * length * rows,
    )(samples, scores)


def expand_kernel(x_ref, scores_ref, out_ref, pair):
    @pl.when(pl.program_id(0) == 0)
    def _():
        pair[...] = jnp.concatenate(split(scores_ref[...]), axis=0)

    width = x_ref.shape[2]
    part = min(PART, width)
    for at in range(0, width, part):
        high, low = split(x_ref[0, :, at : at + part])
        out_ref[at : at + part] = expand_part(pair[...], high, low).T


def expand(samples, group, scores):
    _, length, rows = samples.shape
    size = scores.shape[0]
    width = min(WIDTH, rows)
    return call(
        expand_kernel,
        (rows // width,),
        [
            pl.BlockSpec((1, length, width), lambda i: (group, 0, i)),
            pl.BlockSpec((size, length), lambda i: (0, 0)),
        ],
        pl.BlockSpec((width, size), lambda i: (i, 0)),
        jax.ShapeDtypeStruct((rows, size), jnp.float32),
        [pltpu.VMEM((2 * size, length), jnp.bfloat16)],
        8 * length * rows * size,
        4 * length * rows,
    )(samples, scores)


def normal_kernel(width_all, first_ref, second_ref, out_ref, start_ref):
    gram = dot_exact(first_ref[...], second_ref[...], ((1,), (0,))) * (1.0 / width_all)
    (inverse,) = inverse_factors([gram])
    scores = dot_exact(inverse, second_ref[...], ((1,), (1,)))
    out_ref[...] = scores
    start_ref[...] = dot_exact(scores, first_ref[...], ((1,), (1,)))


def normalise(first, second, width_all):
    size, length = first.shape
    return pl.pallas_call(
        functools.partial(normal_kernel, width_all),
        out_shape=(
            jax.ShapeDtypeStruct((size, length), jnp.float32),
            jax.ShapeDtypeStruct((size, size), jnp.float32),
        ),
        compiler_params=pltpu.CompilerParams(vmem_limit_bytes=40 * MEGA),
        cost_estimate=pl.CostEstimate(
            flops=4_000_000_000, bytes_accessed=4 * 3 * size * length, transcendentals=0
        ),
    )(first, second)


def gram_kernel(own0, own1, other0, other1, out_ref):
    @pl.when(pl.program_id(0) == 0)
    def _():
        out_ref[...] = jnp.zeros_like(out_ref)

    size = own0.shape[1]
    first = ((0,), (0,))
    a, b = own0[...], own1[...]
    row = dot_exact(a, jnp.concatenate([a, b], axis=1), first)
    out_ref[0] += row[:, :size]
    out_ref[1] += row[:, size:]
    out_ref[2] += dot_exact(b, b, first)
    swap = lax.rem(lax.axis_index("sample"), 2) == 1
    c, d = other0[...], other1[...]
    out_ref[3] += dot_exact(a, jnp.where(swap, d, c), first)
    out_ref[4] += dot_exact(b, jnp.where(swap, c, d), first)


def partial_grams(own, other):
    rows, size = own[0].shape
    height = min(ROWS, rows)
    return call(
        gram_kernel,
        (rows // height,),
        [pl.BlockSpec((height, size), lambda i: (i, 0))] * 4,
        pl.BlockSpec((5, size, size), lambda i: (0, 0, 0)),
        jax.ShapeDtypeStruct((5, size, size), jnp.float32),
        [],
        2 * 30 * rows * size * size,
        4 * 4 * rows * size,
    )(*own, *other)


def final_kernel(width_all, first, second, start0, start1, inverse_ref, out_ref, gram, matrix, block):
    count, size, _ = inverse_ref.shape
    at = lambda g: slice(g * size, (g + 1) * size)
    places = (
        (first, ((0, 0), (0, 1), (1, 1), (0, 2), (1, 3))),
        (second, ((2, 2), (2, 3), (3, 3), (2, 1), (3, 0))),
    )
    for parts, where in places:
        for k, (g, h) in enumerate(where):
            gram[at(g), at(h)] = parts[k]
            if g != h:
                gram[at(h), at(g)] = parts[k].T
    inverses = inverse_factors(
        [gram[at(g), at(g)] * (1.0 / width_all) for g in range(count)]
    )
    starts = [start0[0], start0[1], start1[0], start1[1]]
    for g in range(count):
        inverse_ref[g] = inverses[g]
        block[at(g), :] = dot_exact(inverses[g], starts[g], ((1,), (0,)))
        row = dot_exact(inverses[g], gram[at(g), :], ((1,), (0,)))
        for h in range(count):
            matrix[at(g), at(h)] = dot_exact(row[:, at(h)], inverses[h], ((1,), (1,)))

    def step(_, carry):
        held = block[...] * (1.0 / count)
        product = dot_exact(matrix[...], held, ((1,), (0,)))
        small = dot_exact(held, product, ((0,), (0,))) * (1.0 / width_all)
        (inverse,) = inverse_factors([small])
        weights = dot_exact(held, inverse, ((1,), (1,)))
        for g in range(count):
            out_ref[g] = weights[at(g)]
        block[...] = dot_exact(product, inverse, ((1,), (1,)))
        return carry

    lax.fori_loop(0, FINAL_ITERS, step, 0)
    for g in range(count):
        out_ref[g] = dot_exact(inverse_ref[g], out_ref[g], ((0,), (0,)))


def final_iterations(first, second, start0, start1, width_all):
    size = first.shape[-1]
    groups_all = 4
    out = jax.ShapeDtypeStruct((groups_all, size, size), jnp.float32)
    return pl.pallas_call(
        functools.partial(final_kernel, width_all),
        out_shape=(out, out),
        scratch_shapes=[
            pltpu.VMEM((groups_all * size, groups_all * size), jnp.float32),
            pltpu.VMEM((groups_all * size, groups_all * size), jnp.float32),
            pltpu.VMEM((groups_all * size, size), jnp.float32),
        ],
        compiler_params=pltpu.CompilerParams(vmem_limit_bytes=40 * MEGA),
    )(first, second, start0, start1)


def output_kernel(own0, own1, other0, other1, inverse_ref, weight_ref, panel_ref, out_ref, sides):
    size = own0.shape[1]
    core = lax.rem(lax.axis_index("sample"), 2)

    @pl.when(pl.program_id(0) == 0)
    def _():
        def side(value, slot):
            high, low = split(value)
            sides[slot, :size, :size] = high
            sides[slot, :size, size:] = low
            sides[slot, size:, :size] = high
            sides[slot, size:, size:] = jnp.zeros_like(low)

        for g in range(2):
            side(inverse_ref[2 * core + g].T, g)
            side(weight_ref[2 * core + g], 2 + g)
            side(weight_ref[2 * (1 - core) + g], 4 + g)

    def product(halves, slot):
        both = dot_short(halves, sides[slot])
        return both[:, :size] + both[:, size:]

    sums = []
    for k, pair in enumerate(((own0, own1), (other0, other1))):
        parts = []
        for g in range(2):
            halves = jnp.concatenate(split(pair[g][...]), axis=1)
            if k == 0:
                panel_ref[g] = product(halves, g)
            parts.append(product(halves, 2 * (k + 1) + g))
        sums.append(parts[0] + parts[1])
    out_ref[...] = sums[0] + sums[1]


def outputs(own, other, inverses, weights):
    rows, size = own[0].shape
    height = min(ROWS, rows)
    whole = pl.BlockSpec(inverses.shape, lambda i: (0, 0, 0))
    return call(
        output_kernel,
        (rows // height,),
        [pl.BlockSpec((height, size), lambda i: (i, 0))] * 4 + [whole, whole],
        (
            pl.BlockSpec((2, height, size), lambda i: (0, i, 0)),
            pl.BlockSpec((height, size), lambda i: (i, 0)),
        ),
        (
            jax.ShapeDtypeStruct((2, rows, size), jnp.float32),
            jax.ShapeDtypeStruct((rows, size), jnp.float32),
        ),
        [pltpu.VMEM((6, 2 * size, 2 * size), jnp.bfloat16)],
        2 * 24 * rows * size * size,
        4 * 7 * rows * size,
    )(*own, *other, inverses, weights)


def bit_orders(bits):
    return [list(range(bits)), list(range(1, bits)) + [0]]


def total_over_assets(value):
    count, cores = lax.axis_size("asset"), lax.axis_size("sample")
    bits = count.bit_length() - 1
    orders = bit_orders(bits)
    place, core = lax.axis_index("asset"), lax.axis_index("sample")

    def exchange(held, stage):
        pairs = [
            (a * cores + c, (a ^ (1 << orders[c % 2][stage])) * cores + c)
            for a in range(count)
            for c in range(cores)
        ]
        return lax.ppermute(held, ("asset", "sample"), pairs)

    def my_bit(stage):
        bit = jnp.where(core % 2 == 0, orders[0][stage], orders[1][stage])
        return (place >> bit) & 1

    shape = value.shape
    held = value.reshape((-1, shape[-1]))
    for stage in range(bits):
        halves = held.reshape((2, -1, shape[-1]))
        mine = my_bit(stage)
        sent = lax.dynamic_index_in_dim(halves, 1 - mine, 0, keepdims=False)
        kept = lax.dynamic_index_in_dim(halves, mine, 0, keepdims=False)
        held = kept + exchange(sent, stage)
    for stage in reversed(range(bits)):
        other = exchange(held, stage)
        mine = my_bit(stage)
        held = jnp.where(
            mine == 0,
            jnp.concatenate([held, other], axis=0),
            jnp.concatenate([other, held], axis=0),
        )
    return held.reshape(shape)


def total_direct(value):
    count = lax.axis_size("asset")
    place = lax.axis_index("asset")
    shape = value.shape
    parts = value.reshape((count, -1, shape[-1]))
    part = lambda index: lax.dynamic_index_in_dim(parts, index % count, 0, keepdims=False)
    ring = lambda held, d: lax.ppermute(
        held, "asset", [(a, (a + d) % count) for a in range(count)]
    )
    total = part(place)
    for received in [ring(part(place + d), d) for d in range(1, count)]:
        total = total + received
    arrived = [total] + [ring(total, d) for d in range(1, count)]
    turned = jnp.stack(arrived[::-1] + arrived[::-1], axis=0)
    whole = lax.dynamic_slice_in_dim(turned, count - 1 - place, count, axis=0)
    return whole.reshape(shape)


def shards(samples, start_panel):
    rows, size = start_panel.shape
    width_all = rows * lax.axis_size("asset")
    groups = range(samples.shape[0])
    core = lax.axis_index("sample")
    swap = lambda held: lax.ppermute(held, "sample", [(0, 1), (1, 0)])

    first = [total_over_assets(project(samples, g, start_panel)) for g in groups]
    following = [total_over_assets(apply(samples, g, first[g])) for g in groups]
    normal = [normalise(first[g], following[g], width_all) for g in groups]
    own = [expand(samples, g, normal[g][0]) for g in groups]
    starts = jnp.stack([normal[g][1] for g in groups])
    other_starts = swap(starts)
    other = [swap(own[g]) for g in groups]
    grams = total_direct(partial_grams(own, other))
    other_grams = swap(grams)
    ordered = lambda a, b: (jnp.where(core == 0, a, b), jnp.where(core == 0, b, a))
    inverses, weights = final_iterations(
        *ordered(grams, other_grams), *ordered(starts, other_starts), width_all
    )
    return outputs(own, other, inverses, weights)


def solution(mesh):
    placed = (P(("rep", "sample"), None, "asset"), P("asset", None))
    return jax.shard_map(
        shards,
        mesh=mesh,
        in_specs=placed,
        out_specs=(P(("rep", "sample"), "asset", None), P(("rep", "asset"), None)),
        check_vma=False,
    )
```

```python
import functools

import jax
import jax.numpy as jnp
from jax import lax
from jax.experimental import pallas as pl
from jax.experimental.pallas import tpu as pltpu
from jax.sharding import PartitionSpec as P

LOCAL_ITERS = 2
FINAL_ITERS = 4


HIGH = lax.Precision.HIGHEST
TILE = 8
PANEL = 4
WIDTH = 512
ROWS = 1024
MEGA = 1024 * 1024


def dot_exact(left, right, dims):
    return lax.dot_general(
        left, right, (dims, ((), ())), precision=HIGH, preferred_element_type=jnp.float32
    )


def inverse_factors(matrices):
    size = matrices[0].shape[0]
    blocks = size // TILE
    full = (TILE, size)
    sublane = lax.broadcasted_iota(jnp.int32, full, 0)
    lane = lax.broadcasted_iota(jnp.int32, full, 1)
    left, right = [], []
    for matrix in matrices:
        symmetric = 0.5 * (matrix + matrix.T)
        left.append([symmetric[TILE * i : TILE * (i + 1)] for i in range(blocks)])
        right.append(
            [jnp.where(lane == sublane + TILE * i, 1.0, 0.0) for i in range(blocks)]
        )
    along = lambda block, row: jnp.broadcast_to(block[row : row + 1], full)
    across = lambda block, column: jnp.broadcast_to(block[:, column : column + 1], full)
    for panel in range(0, blocks, PANEL):
        last = panel + PANEL
        for j in range(panel, last):
            for a, b in zip(left, right):
                columns = [across(a[j], TILE * j + k) for k in range(TILE)]
                d = [[along(columns[k], i) for k in range(i + 1)] for i in range(TILE)]
                scale = []
                for k in range(TILE):
                    scale.append(lax.rsqrt(d[k][k]))
                    for i in range(k + 1, TILE):
                        d[i][k] = d[i][k] * scale[k]
                    for i in range(k + 1, TILE):
                        for m in range(k + 1, i + 1):
                            d[i][m] = d[i][m] - d[i][k] * d[m][k]

                def substitute(parts):
                    for k in range(TILE):
                        for m in range(k):
                            parts[k] = parts[k] - d[k][m] * parts[m]
                        parts[k] = parts[k] * scale[k]
                    return parts

                rows_a = substitute([along(a[j], k) for k in range(TILE)])
                rows_b = substitute([along(b[j], k) for k in range(TILE)])
                for i in range(j + 1, last):
                    weights = substitute([across(a[i], TILE * j + k) for k in range(TILE)])
                    for k in range(TILE):
                        a[i] = a[i] - weights[k] * rows_a[k]
                        b[i] = b[i] - weights[k] * rows_b[k]

                def gather(rows):
                    block = rows[0]
                    for k in range(1, TILE):
                        block = jnp.where(sublane == k, rows[k], block)
                    return block

                a[j], b[j] = gather(rows_a), gather(rows_b)
        if last < blocks:
            for a, b in zip(left, right):
                top_a = jnp.concatenate(a[panel:last], axis=0)
                top_b = jnp.concatenate(b[panel:last], axis=0)
                change = dot_exact(
                    top_a[:, TILE * last :],
                    jnp.concatenate([top_a, top_b], axis=1),
                    ((0,), (0,)),
                )
                for i in range(last, blocks):
                    rows = change[TILE * (i - last) : TILE * (i - last + 1)]
                    a[i] = a[i] - rows[:, :size]
                    b[i] = b[i] - rows[:, size:]
    return [jnp.concatenate(b, axis=0) for b in right]


def split(value):
    high = value.astype(jnp.bfloat16)
    return high, (value - high.astype(jnp.float32)).astype(jnp.bfloat16)


def dot_short(left, right, dims=((1,), (0,))):
    return lax.dot_general(left, right, (dims, ((), ())), preferred_element_type=jnp.float32)


def call(body, grid, in_specs, out_specs, out_shape, scratch, flops, read):
    return pl.pallas_call(
        body,
        grid=grid,
        in_specs=in_specs,
        out_specs=out_specs,
        out_shape=out_shape,
        scratch_shapes=scratch,
        compiler_params=pltpu.CompilerParams(vmem_limit_bytes=52 * MEGA),
        cost_estimate=pl.CostEstimate(flops=flops, bytes_accessed=read, transcendentals=0),
    )


TOKEN = pl.BlockSpec(memory_space=pl.ANY)


def project_kernel(x_ref, panel_ref, token_ref, out_ref, high_ref, low_ref, total):
    step = pl.program_id(0)
    size = panel_ref.shape[1]

    @pl.when(step == 0)
    def _():
        total[...] = jnp.zeros_like(total)

    high, low = split(x_ref[0])
    high_ref[...] = high
    low_ref[...] = low
    panel_high, panel_low = split(panel_ref[...])
    sides = jnp.concatenate(
        [
            jnp.concatenate([panel_high, panel_low], axis=1),
            jnp.concatenate([panel_high, jnp.zeros_like(panel_low)], axis=1),
        ],
        axis=0,
    )
    total[...] += dot_short(jnp.concatenate([high, low], axis=1), sides)

    @pl.when(step == pl.num_programs(0) - 1)
    def _():
        out_ref[...] = (total[:, :size] + total[:, size:]).T


def project(samples, group, panel, slices, index, token):
    _, length, rows = samples.shape
    size = panel.shape[1]
    width = min(WIDTH, rows)
    steps = rows // width // slices
    first = steps * index
    halves = jax.ShapeDtypeStruct((length, steps * width), jnp.bfloat16)
    return call(
        project_kernel,
        (steps,),
        [
            pl.BlockSpec((1, length, width), lambda i: (group, 0, first + i)),
            pl.BlockSpec((width, size), lambda i: (first + i, 0)),
            TOKEN,
        ],
        (
            pl.BlockSpec((size, length), lambda i: (0, 0)),
            pl.BlockSpec((length, width), lambda i: (0, i)),
            pl.BlockSpec((length, width), lambda i: (0, i)),
        ),
        (jax.ShapeDtypeStruct((size, length), jnp.float32), halves, halves),
        [pltpu.VMEM((length, 2 * size), jnp.float32)],
        8 * length * steps * width * size,
        8 * length * steps * width,
    )(samples, panel, token)


def expand_part(pair, high, low):
    size = pair.shape[0] // 2
    both = dot_short(pair, high)
    return (both[:size] + both[size:]) + dot_short(pair[:size], low)


def apply_kernel(high_ref, low_ref, scores_ref, token_ref, out_ref, pair, total):
    step = pl.program_id(0)
    size = scores_ref.shape[0]

    @pl.when(step == 0)
    def _():
        pair[...] = jnp.concatenate(split(scores_ref[...]), axis=0)
        total[...] = jnp.zeros_like(total)

    high, low = high_ref[...], low_ref[...]
    top, rest = split(expand_part(pair[...], high, low))
    sides = jnp.concatenate(
        [
            jnp.concatenate([top, rest], axis=0),
            jnp.concatenate([top, jnp.zeros_like(rest)], axis=0),
        ],
        axis=1,
    )
    total[...] += dot_short(jnp.concatenate([high, low], axis=1), sides, ((1,), (1,)))

    @pl.when(step == pl.num_programs(0) - 1)
    def _():
        out_ref[...] = total[:, :size] + total[:, size:]


def apply(halves, scores, token):
    length, rows = halves[0].shape
    size = scores.shape[0]
    width = min(WIDTH, rows)
    block = pl.BlockSpec((length, width), lambda i: (0, i))
    return call(
        apply_kernel,
        (rows // width,),
        [block, block, pl.BlockSpec((size, length), lambda i: (0, 0)), TOKEN],
        pl.BlockSpec((length, size), lambda i: (0, 0)),
        jax.ShapeDtypeStruct((length, size), jnp.float32),
        [
            pltpu.VMEM((2 * size, length), jnp.bfloat16),
            pltpu.VMEM((length, 2 * size), jnp.float32),
        ],
        16 * length * rows * size,
        4 * length * rows,
    )(*halves, scores, token)


def expand_kernel(*refs):
    *halves, scores_ref, token_ref, out_ref, pair = refs
    step = pl.program_id(0)

    @pl.when(step == 0)
    def _():
        pair[...] = jnp.concatenate(split(scores_ref[...]), axis=0)

    slices = len(halves) // 2
    for index in range(slices):

        @pl.when(step // (pl.num_programs(0) // slices) == index)
        def _():
            high, low = halves[2 * index][...], halves[2 * index + 1][...]
            out_ref[...] = expand_part(pair[...], high, low).T


def expand(halves, scores, token):
    slices = len(halves)
    length, held = halves[0][0].shape
    size = scores.shape[0]
    width = min(WIDTH, held)
    steps = held // width
    blocks = [
        pl.BlockSpec(
            (length, width),
            lambda i, index=index: (0, jnp.clip(i - index * steps, 0, steps - 1)),
        )
        for index in range(slices)
        for _ in range(2)
    ]
    return call(
        expand_kernel,
        (steps * slices,),
        [*blocks, pl.BlockSpec((size, length), lambda i: (0, 0)), TOKEN],
        pl.BlockSpec((width, size), lambda i: (i, 0)),
        jax.ShapeDtypeStruct((held * slices, size), jnp.float32),
        [pltpu.VMEM((2 * size, length), jnp.bfloat16)],
        8 * length * held * slices * size,
        4 * length * held * slices,
    )(*[half for pair in halves for half in pair], scores, token)


def normal_kernel(width_all, first_ref, second_ref, token_ref, out_ref):
    gram = dot_exact(first_ref[...], second_ref[...], ((1,), (0,))) * (1.0 / width_all)
    (inverse,) = inverse_factors([gram])
    out_ref[...] = dot_exact(inverse, second_ref[...], ((1,), (1,)))


def normalise(first, second, width_all, token):
    size, length = first.shape
    whole = lambda held: pl.BlockSpec(held.shape, lambda: (0, 0))
    return pl.pallas_call(
        functools.partial(normal_kernel, width_all),
        in_specs=[whole(first), whole(second), TOKEN],
        out_specs=whole(first),
        out_shape=jax.ShapeDtypeStruct((size, length), jnp.float32),
        compiler_params=pltpu.CompilerParams(vmem_limit_bytes=40 * MEGA),
        cost_estimate=pl.CostEstimate(
            flops=6_000_000_000, bytes_accessed=4 * 3 * size * length, transcendentals=0
        ),
    )(first, second, token)


def own_gram_kernel(own0, own1, out_ref):
    @pl.when(pl.program_id(0) == 0)
    def _():
        out_ref[...] = jnp.zeros_like(out_ref)

    size = own0.shape[1]
    first = ((0,), (0,))
    high, low = split(jnp.concatenate([own0[...], own1[...]], axis=1))
    both = dot_short(high, jnp.concatenate([high, low], axis=1), first)
    mixed = both[:, 2 * size :]
    gram = both[:, : 2 * size] + (dot_short(low, low, first) + (mixed + mixed.T))
    out_ref[0] += gram[:size, :size]
    out_ref[1] += gram[:size, size:]
    out_ref[2] += gram[size:, size:]


def cross_gram_kernel(own0, own1, other0, other1, out_ref):
    @pl.when(pl.program_id(0) == 0)
    def _():
        out_ref[...] = jnp.zeros_like(out_ref)

    size = own0.shape[1]
    swapped = lax.rem(lax.axis_index("sample"), 2) == 1
    c, d = other0[...], other1[...]
    pairs = ((own0[...], jnp.where(swapped, d, c)), (own1[...], jnp.where(swapped, c, d)))
    for k, (left, right) in enumerate(pairs):
        both = dot_short(
            jnp.concatenate(split(left), axis=1),
            jnp.concatenate(split(right), axis=1),
            ((0,), (0,)),
        )
        out_ref[k] += (both[:size, :size] + both[size:, size:]) + (
            both[:size, size:] + both[size:, :size]
        )


def partial_grams(body, count, panels):
    rows, size = panels[0].shape
    height = min(ROWS, rows)
    return call(
        body,
        (rows // height,),
        [pl.BlockSpec((height, size), lambda i: (i, 0))] * len(panels),
        pl.BlockSpec((count, size, size), lambda i: (0, 0, 0)),
        jax.ShapeDtypeStruct((count, size, size), jnp.float32),
        [],
        2 * 30 * rows * size * size,
        4 * len(panels) * rows * size,
    )(*panels)


def final_kernel(
    width_all, first, second, start0, start1, inverse_ref, out_ref, gram, matrix, held, product
):
    count, size, _ = inverse_ref.shape
    at = lambda g: slice(g * size, (g + 1) * size)
    places = (
        (first, ((0, 0), (0, 1), (1, 1), (0, 2), (1, 3))),
        (second, ((2, 2), (2, 3), (3, 3), (2, 1), (3, 0))),
    )
    for parts, where in places:
        for k, (g, h) in enumerate(where):
            gram[at(g), at(h)] = parts[k]
            if g != h:
                gram[at(h), at(g)] = parts[k].T
    inverses = inverse_factors(
        [gram[at(g), at(g)] * (1.0 / width_all) for g in range(count)]
    )
    starts = [start0[0], start0[1], start1[0], start1[1]]
    for g in range(count):
        inverse_ref[g] = inverses[g]
        held[at(g), :] = dot_exact(inverses[g] * (1.0 / count), starts[g], ((1,), (0,)))
        gram[at(g), :] = dot_exact(inverses[g], gram[at(g), :], ((1,), (0,)))
    for h in range(count):
        matrix[:, at(h)] = dot_exact(gram[:, at(h)], inverses[h], ((1,), (1,)))
    product[...] = dot_exact(matrix[...], held[...], ((1,), (0,)))

    def step(_, carry):
        small = dot_exact(held[...], product[...], ((0,), (0,))) * (1.0 / width_all)
        following = product[...] * (1.0 / count)
        ahead = dot_exact(matrix[...], following, ((1,), (0,)))
        (inverse,) = inverse_factors([small])
        weights = dot_exact(held[...], inverse, ((1,), (1,)))
        for g in range(count):
            out_ref[g] = weights[at(g)]
        held[...] = dot_exact(following, inverse, ((1,), (1,)))
        product[...] = dot_exact(ahead, inverse, ((1,), (1,)))
        return carry

    lax.fori_loop(0, FINAL_ITERS, step, 0)
    for g in range(count):
        out_ref[g] = dot_exact(inverse_ref[g], out_ref[g], ((0,), (0,)))


def final_iterations(first, second, start0, start1, width_all):
    size = first.shape[-1]
    groups_all = 4
    out = jax.ShapeDtypeStruct((groups_all, size, size), jnp.float32)
    wide = groups_all * size
    return pl.pallas_call(
        functools.partial(final_kernel, width_all),
        out_shape=(out, out),
        scratch_shapes=[
            pltpu.VMEM((wide, wide), jnp.float32),
            pltpu.VMEM((wide, wide), jnp.float32),
            pltpu.VMEM((wide, size), jnp.float32),
            pltpu.VMEM((wide, size), jnp.float32),
        ],
        compiler_params=pltpu.CompilerParams(vmem_limit_bytes=40 * MEGA),
    )(first, second, start0, start1)


def output_kernel(own0, own1, other0, other1, inverse_ref, weight_ref, panel_ref, out_ref, sides):
    size = own0.shape[1]
    core = lax.rem(lax.axis_index("sample"), 2)

    @pl.when(pl.program_id(0) == 0)
    def _():
        def side(value, slot):
            high, low = split(value)
            sides[slot, :size, :size] = high
            sides[slot, :size, size:] = low
            sides[slot, size:, :size] = high
            sides[slot, size:, size:] = jnp.zeros_like(low)

        for g in range(2):
            side(inverse_ref[2 * core + g].T, g)
            side(weight_ref[2 * core + g], 2 + g)
            side(weight_ref[2 * (1 - core) + g], 4 + g)

    def product(halves, slot):
        both = dot_short(halves, sides[slot])
        return both[:, :size] + both[:, size:]

    sums = []
    for k, pair in enumerate(((own0, own1), (other0, other1))):
        parts = []
        for g in range(2):
            halves = jnp.concatenate(split(pair[g][...]), axis=1)
            if k == 0:
                panel_ref[g] = product(halves, g)
            parts.append(product(halves, 2 * (k + 1) + g))
        sums.append(parts[0] + parts[1])
    out_ref[...] = sums[0] + sums[1]


def outputs(own, other, inverses, weights):
    rows, size = own[0].shape
    height = min(ROWS, rows)
    whole = pl.BlockSpec(inverses.shape, lambda i: (0, 0, 0))
    return call(
        output_kernel,
        (rows // height,),
        [pl.BlockSpec((height, size), lambda i: (i, 0))] * 4 + [whole, whole],
        (
            pl.BlockSpec((2, height, size), lambda i: (0, i, 0)),
            pl.BlockSpec((height, size), lambda i: (i, 0)),
        ),
        (
            jax.ShapeDtypeStruct((2, rows, size), jnp.float32),
            jax.ShapeDtypeStruct((rows, size), jnp.float32),
        ),
        [pltpu.VMEM((6, 2 * size, 2 * size), jnp.bfloat16)],
        2 * 24 * rows * size * size,
        4 * 7 * rows * size,
    )(*own, *other, inverses, weights)


class Total:
    def __init__(self, value):
        self.count, self.cores = lax.axis_size("asset"), lax.axis_size("sample")
        self.bits = self.count.bit_length() - 1
        self.orders = [list(range(self.bits)), list(range(1, self.bits)) + [0]]
        self.place, self.core = lax.axis_index("asset"), lax.axis_index("sample")
        self.shape = value.shape
        self.held = value.reshape((-1, value.shape[-1]))
        self.round = 0
        self.start()

    @property
    def rounds(self):
        return 2 * self.bits

    def stage(self):
        return min(self.round, self.rounds - 1 - self.round)

    def mine(self):
        stage = self.stage()
        bit = jnp.where(self.core % 2 == 0, self.orders[0][stage], self.orders[1][stage])
        return (self.place >> bit) & 1

    def start(self):
        stage, mine = self.stage(), self.mine()
        if self.round < self.bits:
            halves = self.held.reshape((2, -1, self.shape[-1]))
            self.sent = lax.dynamic_index_in_dim(halves, 1 - mine, 0, keepdims=False)
            self.kept = lax.dynamic_index_in_dim(halves, mine, 0, keepdims=False)
        else:
            self.sent = self.kept = self.held
        pairs = [
            (a * self.cores + c, (a ^ (1 << self.orders[c % 2][stage])) * self.cores + c)
            for a in range(self.count)
            for c in range(self.cores)
        ]
        self.arriving = lax.ppermute(self.sent, ("asset", "sample"), pairs)

    def step(self):
        if self.round < self.bits:
            self.held = self.kept + self.arriving
        else:
            self.held = jnp.where(
                self.mine() == 0,
                jnp.concatenate([self.kept, self.arriving], axis=0),
                jnp.concatenate([self.arriving, self.kept], axis=0),
            )
        self.round += 1
        if self.round < self.rounds:
            self.start()

    def finish(self):
        while self.round < self.rounds:
            self.step()
        return self.held.reshape(self.shape)


def shards(samples, start_panel):
    rows, size = start_panel.shape
    width_all = rows * lax.axis_size("asset")
    core = lax.axis_index("sample")
    swap = lambda held: lax.ppermute(held, "sample", [(0, 1), (1, 0)])
    steps = rows // min(WIDTH, rows)
    slices = next(n for n in (4, 2, 1) if steps % n == 0)

    def beside(result, total):
        if total.round < total.rounds:
            result, total.arriving = lax.optimization_barrier((result, total.arriving))
        return result

    def in_slices(run, total):
        done = []
        for index in range(slices):
            if index and total.round < total.rounds:
                total.step()
            done.append(beside(run(index, total.sent), total))
        return done

    none = jnp.zeros((8, 128), jnp.float32)
    added = lambda values: functools.reduce(jnp.add, values)
    parts0 = [project(samples, 0, start_panel, 2, k, none) for k in range(2)]
    first0 = Total(added([part[0] for part in parts0]))
    parts1 = in_slices(
        lambda k, token: project(samples, 1, start_panel, slices, k, token), first0
    )
    first1 = Total(added([part[0] for part in parts1]))
    while first0.round < first0.rounds:
        first0.step()
        if first1.round < first1.rounds:
            first1.step()
    halves0 = [part[1:] for part in parts0]
    halves1 = [part[1:] for part in parts1]
    scores0 = first0.finish()
    pieces = []
    for k, half in enumerate(halves0):
        pieces.append(beside(apply(half, scores0, first1.sent), first1))
        first1.step() if first1.round < first1.rounds else None
    scores1 = first1.finish()
    second0 = Total(added(pieces))
    second1 = Total(
        added(in_slices(lambda k, token: apply(halves1[k], scores1, token), second0))
    )
    while second0.round < second0.rounds:
        second0.step()
        if second1.round < second1.rounds - 2:
            second1.step()
    normal0 = beside(normalise(scores0, second0.finish(), width_all, second1.sent), second1)
    second1.step()
    own0 = beside(expand(halves0, normal0, second1.sent), second1)
    other0 = swap(own0)
    normal1 = normalise(scores1, second1.finish(), width_all, own0)
    own1 = expand(halves1, normal1, none)
    other1 = swap(own1)
    starts = jnp.einsum(
        "gks,gls->gkl",
        jnp.stack([normal0, normal1]),
        jnp.stack([scores0, scores1]),
        precision=HIGH,
    )
    other_starts = swap(starts)
    grams = jnp.concatenate(
        [
            partial_grams(own_gram_kernel, 3, (own0, own1)),
            partial_grams(cross_gram_kernel, 2, (own0, own1, other0, other1)),
        ]
    )
    grams = Total(grams).finish()
    other_grams = swap(grams)
    ordered = lambda a, b: (jnp.where(core == 0, a, b), jnp.where(core == 0, b, a))
    inverses, weights = final_iterations(
        *ordered(grams, other_grams), *ordered(starts, other_starts), width_all
    )
    return outputs((own0, own1), (other0, other1), inverses, weights)


def solution(mesh):
    placed = (P(("rep", "sample"), None, "asset"), P("asset", None))
    return jax.shard_map(
        shards,
        mesh=mesh,
        in_specs=placed,
        out_specs=(P(("rep", "sample"), "asset", None), P(("rep", "asset"), None)),
        check_vma=False,
    )
```

```python
import functools

import jax
import jax.numpy as jnp
from jax import lax
from jax.experimental import pallas as pl
from jax.experimental.pallas import tpu as pltpu
from jax.sharding import PartitionSpec as P

LOCAL_ITERS = 2
FINAL_ITERS = 4


HIGH = lax.Precision.HIGHEST
TILE = 8
PANEL = 4
WIDTH = 512
PART = 256
ROWS = 1024
MEGA = 1024 * 1024


def dot_exact(left, right, dims):
    return lax.dot_general(
        left, right, (dims, ((), ())), precision=HIGH, preferred_element_type=jnp.float32
    )


def inverse_factors(matrices):
    size = matrices[0].shape[0]
    blocks = size // TILE
    full = (TILE, size)
    sublane = lax.broadcasted_iota(jnp.int32, full, 0)
    lane = lax.broadcasted_iota(jnp.int32, full, 1)
    left, right = [], []
    for matrix in matrices:
        symmetric = 0.5 * (matrix + matrix.T)
        left.append([symmetric[TILE * i : TILE * (i + 1)] for i in range(blocks)])
        right.append(
            [jnp.where(lane == sublane + TILE * i, 1.0, 0.0) for i in range(blocks)]
        )
    along = lambda block, row: jnp.broadcast_to(block[row : row + 1], full)
    across = lambda block, column: jnp.broadcast_to(block[:, column : column + 1], full)
    for panel in range(0, blocks, PANEL):
        last = panel + PANEL
        for j in range(panel, last):
            for a, b in zip(left, right):
                columns = [across(a[j], TILE * j + k) for k in range(TILE)]
                d = [[along(columns[k], i) for k in range(i + 1)] for i in range(TILE)]
                scale = []
                for k in range(TILE):
                    scale.append(lax.rsqrt(d[k][k]))
                    for i in range(k + 1, TILE):
                        d[i][k] = d[i][k] * scale[k]
                    for i in range(k + 1, TILE):
                        for m in range(k + 1, i + 1):
                            d[i][m] = d[i][m] - d[i][k] * d[m][k]

                def substitute(parts):
                    for k in range(TILE):
                        for m in range(k):
                            parts[k] = parts[k] - d[k][m] * parts[m]
                        parts[k] = parts[k] * scale[k]
                    return parts

                rows_a = substitute([along(a[j], k) for k in range(TILE)])
                rows_b = substitute([along(b[j], k) for k in range(TILE)])
                for i in range(j + 1, last):
                    weights = substitute([across(a[i], TILE * j + k) for k in range(TILE)])
                    for k in range(TILE):
                        a[i] = a[i] - weights[k] * rows_a[k]
                        b[i] = b[i] - weights[k] * rows_b[k]

                def gather(rows):
                    block = rows[0]
                    for k in range(1, TILE):
                        block = jnp.where(sublane == k, rows[k], block)
                    return block

                a[j], b[j] = gather(rows_a), gather(rows_b)
        if last < blocks:
            for a, b in zip(left, right):
                top_a = jnp.concatenate(a[panel:last], axis=0)
                top_b = jnp.concatenate(b[panel:last], axis=0)
                change = dot_exact(
                    top_a[:, TILE * last :],
                    jnp.concatenate([top_a, top_b], axis=1),
                    ((0,), (0,)),
                )
                for i in range(last, blocks):
                    rows = change[TILE * (i - last) : TILE * (i - last + 1)]
                    a[i] = a[i] - rows[:, :size]
                    b[i] = b[i] - rows[:, size:]
    return [jnp.concatenate(b, axis=0) for b in right]


def split(value):
    high = value.astype(jnp.bfloat16)
    return high, (value - high.astype(jnp.float32)).astype(jnp.bfloat16)


def dot_short(left, right, dims=((1,), (0,))):
    return lax.dot_general(left, right, (dims, ((), ())), preferred_element_type=jnp.float32)


def call(body, grid, in_specs, out_specs, out_shape, scratch, flops, read, aliases={}):
    return pl.pallas_call(
        body,
        grid=grid,
        in_specs=in_specs,
        out_specs=out_specs,
        out_shape=out_shape,
        scratch_shapes=scratch,
        input_output_aliases=aliases,
        compiler_params=pltpu.CompilerParams(vmem_limit_bytes=52 * MEGA),
        cost_estimate=pl.CostEstimate(flops=flops, bytes_accessed=read, transcendentals=0),
    )


TOKEN = pl.BlockSpec(memory_space=pl.ANY)


def project_kernel(x_ref, panel_ref, token_ref, out_ref, total):
    step = pl.program_id(0)
    size = panel_ref.shape[1]

    @pl.when(step == 0)
    def _():
        total[...] = jnp.zeros_like(total)

    high, low = split(x_ref[0])
    panel_high, panel_low = split(panel_ref[...])
    sides = jnp.concatenate(
        [
            jnp.concatenate([panel_high, panel_low], axis=1),
            jnp.concatenate([panel_high, jnp.zeros_like(panel_low)], axis=1),
        ],
        axis=0,
    )
    total[...] += dot_short(jnp.concatenate([high, low], axis=1), sides)

    @pl.when(step == pl.num_programs(0) - 1)
    def _():
        out_ref[...] = (total[:, :size] + total[:, size:]).T


def project(samples, group, panel, slices, index, token):
    _, length, rows = samples.shape
    size = panel.shape[1]
    width = min(WIDTH, rows)
    steps = rows // width // slices
    first = steps * index
    return call(
        project_kernel,
        (steps,),
        [
            pl.BlockSpec((1, length, width), lambda i: (group, 0, first + i)),
            pl.BlockSpec((width, size), lambda i: (first + i, 0)),
            TOKEN,
        ],
        pl.BlockSpec((size, length), lambda i: (0, 0)),
        jax.ShapeDtypeStruct((size, length), jnp.float32),
        [pltpu.VMEM((length, 2 * size), jnp.float32)],
        8 * length * steps * width * size,
        4 * length * steps * width,
    )(samples, panel, token)


def expand_part(pair, high, low):
    size = pair.shape[0] // 2
    both = dot_short(pair, high)
    return (both[:size] + both[size:]) + dot_short(pair[:size], low)


def apply_kernel(x_ref, scores_ref, token_ref, out_ref, pair, total):
    step = pl.program_id(0)
    size = scores_ref.shape[0]

    @pl.when(step == 0)
    def _():
        pair[...] = jnp.concatenate(split(scores_ref[...]), axis=0)
        total[...] = jnp.zeros_like(total)

    width = x_ref.shape[2]
    part = min(PART, width)
    halves = [split(x_ref[0, :, at : at + part]) for at in range(0, width, part)]
    expanded = [split(expand_part(pair[...], high, low)) for high, low in halves]
    tops = [top for top, _ in expanded]
    rests = [rest for _, rest in expanded]
    sides = jnp.concatenate(
        [
            jnp.concatenate(tops + tops, axis=1),
            jnp.concatenate(rests + [jnp.zeros_like(rest) for rest in rests], axis=1),
        ],
        axis=0,
    )
    left = jnp.concatenate([high for high, _ in halves] + [low for _, low in halves], axis=1)
    total[...] += dot_short(left, sides, ((1,), (1,)))

    @pl.when(step == pl.num_programs(0) - 1)
    def _():
        out_ref[...] = total[:, :size] + total[:, size:]


def apply(samples, group, scores, slices, index, token):
    _, length, rows = samples.shape
    size = scores.shape[0]
    width = min(WIDTH, rows)
    steps = rows // width // slices
    first = steps * index
    return call(
        apply_kernel,
        (steps,),
        [
            pl.BlockSpec((1, length, width), lambda i: (group, 0, first + i)),
            pl.BlockSpec((size, length), lambda i: (0, 0)),
            TOKEN,
        ],
        pl.BlockSpec((length, size), lambda i: (0, 0)),
        jax.ShapeDtypeStruct((length, size), jnp.float32),
        [
            pltpu.VMEM((2 * size, length), jnp.bfloat16),
            pltpu.VMEM((length, 2 * size), jnp.float32),
        ],
        16 * length * steps * width * size,
        4 * length * steps * width,
    )(samples, scores, token)


def expand_kernel(x_ref, scores_ref, token_ref, *rest):
    out_ref, pair = rest[-2:]

    @pl.when(pl.program_id(0) == 0)
    def _():
        pair[...] = jnp.concatenate(split(scores_ref[...]), axis=0)

    width = x_ref.shape[2]
    part = min(PART, width)
    for at in range(0, width, part):
        high, low = split(x_ref[0, :, at : at + part])
        out_ref[at : at + part] = expand_part(pair[...], high, low).T


def expand(samples, group, scores, slices, index, token, before=None):
    _, length, rows = samples.shape
    size = scores.shape[0]
    width = min(WIDTH, rows)
    steps = rows // width // slices
    first = steps * index
    earlier = [] if before is None else [before]
    return call(
        expand_kernel,
        (steps,),
        [
            pl.BlockSpec((1, length, width), lambda i: (group, 0, first + i)),
            pl.BlockSpec((size, length), lambda i: (0, 0)),
            TOKEN,
            *[TOKEN for _ in earlier],
        ],
        pl.BlockSpec((width, size), lambda i: (first + i, 0)),
        jax.ShapeDtypeStruct((rows, size), jnp.float32),
        [pltpu.VMEM((2 * size, length), jnp.bfloat16)],
        8 * length * steps * width * size,
        4 * length * steps * width,
        {3: 0} if earlier else {},
    )(samples, scores, token, *earlier)


def normal_kernel(width_all, first_ref, second_ref, token_ref, out_ref):
    gram = dot_exact(first_ref[...], second_ref[...], ((1,), (0,))) * (1.0 / width_all)
    (inverse,) = inverse_factors([gram])
    out_ref[...] = dot_exact(inverse, second_ref[...], ((1,), (1,)))


def normalise(first, second, width_all, token):
    size, length = first.shape
    whole = lambda held: pl.BlockSpec(held.shape, lambda: (0, 0))
    return pl.pallas_call(
        functools.partial(normal_kernel, width_all),
        in_specs=[whole(first), whole(second), TOKEN],
        out_specs=whole(first),
        out_shape=jax.ShapeDtypeStruct((size, length), jnp.float32),
        compiler_params=pltpu.CompilerParams(vmem_limit_bytes=40 * MEGA),
        cost_estimate=pl.CostEstimate(
            flops=6_000_000_000, bytes_accessed=4 * 3 * size * length, transcendentals=0
        ),
    )(first, second, token)


def own_gram_kernel(own0, own1, out_ref):
    @pl.when(pl.program_id(0) == 0)
    def _():
        out_ref[...] = jnp.zeros_like(out_ref)

    size = own0.shape[1]
    first = ((0,), (0,))
    high, low = split(jnp.concatenate([own0[...], own1[...]], axis=1))
    both = dot_short(high, jnp.concatenate([high, low], axis=1), first)
    mixed = both[:, 2 * size :]
    gram = both[:, : 2 * size] + (dot_short(low, low, first) + (mixed + mixed.T))
    out_ref[0] += gram[:size, :size]
    out_ref[1] += gram[:size, size:]
    out_ref[2] += gram[size:, size:]


def cross_gram_kernel(own0, own1, other0, other1, out_ref, total):
    step = pl.program_id(0)

    @pl.when(step == 0)
    def _():
        total[...] = jnp.zeros_like(total)

    size = own0.shape[1]
    first = ((0,), (0,))
    high, low = split(jnp.concatenate([own0[...], own1[...]], axis=1))
    right, rest = split(jnp.concatenate([other0[...], other1[...]], axis=1))
    both = dot_short(high, jnp.concatenate([right, rest], axis=1), first)
    total[...] += both[:, : 2 * size] + (both[:, 2 * size :] + dot_short(low, right, first))

    @pl.when(step == pl.num_programs(0) - 1)
    def _():
        swapped = lax.rem(lax.axis_index("sample"), 2) == 1
        pick = lambda rows, a, b: jnp.where(swapped, total[rows, b], total[rows, a])
        front, back = slice(0, size), slice(size, 2 * size)
        out_ref[0] = pick(front, front, back)
        out_ref[1] = pick(back, back, front)


def partial_grams(body, count, panels, scratch):
    rows, size = panels[0].shape
    height = min(ROWS, rows)
    return call(
        body,
        (rows // height,),
        [pl.BlockSpec((height, size), lambda i: (i, 0))] * len(panels),
        pl.BlockSpec((count, size, size), lambda i: (0, 0, 0)),
        jax.ShapeDtypeStruct((count, size, size), jnp.float32),
        scratch,
        2 * 30 * rows * size * size,
        4 * len(panels) * rows * size,
    )(*panels)


def final_kernel(
    width_all, first, second, start0, start1, inverse_ref, out_ref, gram, matrix, held, product
):
    count, size, _ = inverse_ref.shape
    at = lambda g: slice(g * size, (g + 1) * size)
    places = (
        (first, ((0, 0), (0, 1), (1, 1), (0, 2), (1, 3))),
        (second, ((2, 2), (2, 3), (3, 3), (2, 1), (3, 0))),
    )
    for parts, where in places:
        for k, (g, h) in enumerate(where):
            gram[at(g), at(h)] = parts[k]
            if g != h:
                gram[at(h), at(g)] = parts[k].T
    inverses = inverse_factors(
        [gram[at(g), at(g)] * (1.0 / width_all) for g in range(count)]
    )
    starts = [start0[0], start0[1], start1[0], start1[1]]
    for g in range(count):
        inverse_ref[g] = inverses[g]
        held[at(g), :] = dot_exact(inverses[g] * (1.0 / count), starts[g], ((1,), (0,)))
        gram[at(g), :] = dot_exact(inverses[g], gram[at(g), :], ((1,), (0,)))
    for h in range(count):
        matrix[:, at(h)] = dot_exact(gram[:, at(h)], inverses[h], ((1,), (1,)))
    product[...] = dot_exact(matrix[...], held[...], ((1,), (0,)))

    def step(_, carry):
        small = dot_exact(held[...], product[...], ((0,), (0,))) * (1.0 / width_all)
        following = product[...] * (1.0 / count)
        ahead = dot_exact(matrix[...], following, ((1,), (0,)))
        (inverse,) = inverse_factors([small])
        weights = dot_exact(held[...], inverse, ((1,), (1,)))
        for g in range(count):
            out_ref[g] = weights[at(g)]
        held[...] = dot_exact(following, inverse, ((1,), (1,)))
        product[...] = dot_exact(ahead, inverse, ((1,), (1,)))
        return carry

    lax.fori_loop(0, FINAL_ITERS, step, 0)
    for g in range(count):
        out_ref[g] = dot_exact(inverse_ref[g], out_ref[g], ((0,), (0,)))


def final_iterations(first, second, start0, start1, width_all):
    size = first.shape[-1]
    groups_all = 4
    out = jax.ShapeDtypeStruct((groups_all, size, size), jnp.float32)
    wide = groups_all * size
    return pl.pallas_call(
        functools.partial(final_kernel, width_all),
        out_shape=(out, out),
        scratch_shapes=[
            pltpu.VMEM((wide, wide), jnp.float32),
            pltpu.VMEM((wide, wide), jnp.float32),
            pltpu.VMEM((wide, size), jnp.float32),
            pltpu.VMEM((wide, size), jnp.float32),
        ],
        compiler_params=pltpu.CompilerParams(vmem_limit_bytes=40 * MEGA),
    )(first, second, start0, start1)


def output_kernel(own0, own1, other0, other1, inverse_ref, weight_ref, panel_ref, out_ref, sides):
    size = own0.shape[1]
    core = lax.rem(lax.axis_index("sample"), 2)

    @pl.when(pl.program_id(0) == 0)
    def _():
        def side(value, slot):
            high, low = split(value)
            sides[slot, :size, :size] = high
            sides[slot, :size, size:] = low
            sides[slot, size:, :size] = high
            sides[slot, size:, size:] = jnp.zeros_like(low)

        for g in range(2):
            side(inverse_ref[2 * core + g].T, g)
            side(weight_ref[2 * core + g], 2 + g)
            side(weight_ref[2 * (1 - core) + g], 4 + g)

    def product(halves, slot):
        both = dot_short(halves, sides[slot])
        return both[:, :size] + both[:, size:]

    sums = []
    for k, pair in enumerate(((own0, own1), (other0, other1))):
        parts = []
        for g in range(2):
            halves = jnp.concatenate(split(pair[g][...]), axis=1)
            if k == 0:
                panel_ref[g] = product(halves, g)
            parts.append(product(halves, 2 * (k + 1) + g))
        sums.append(parts[0] + parts[1])
    out_ref[...] = sums[0] + sums[1]


def outputs(own, other, inverses, weights):
    rows, size = own[0].shape
    height = min(ROWS, rows)
    whole = pl.BlockSpec(inverses.shape, lambda i: (0, 0, 0))
    return call(
        output_kernel,
        (rows // height,),
        [pl.BlockSpec((height, size), lambda i: (i, 0))] * 4 + [whole, whole],
        (
            pl.BlockSpec((2, height, size), lambda i: (0, i, 0)),
            pl.BlockSpec((height, size), lambda i: (i, 0)),
        ),
        (
            jax.ShapeDtypeStruct((2, rows, size), jnp.float32),
            jax.ShapeDtypeStruct((rows, size), jnp.float32),
        ),
        [pltpu.VMEM((6, 2 * size, 2 * size), jnp.bfloat16)],
        2 * 24 * rows * size * size,
        4 * 7 * rows * size,
    )(*own, *other, inverses, weights)


class Total:
    def __init__(self, value):
        self.count, self.cores = lax.axis_size("asset"), lax.axis_size("sample")
        self.bits = self.count.bit_length() - 1
        self.orders = [list(range(self.bits)), list(range(1, self.bits)) + [0]]
        self.place, self.core = lax.axis_index("asset"), lax.axis_index("sample")
        self.shape = value.shape
        self.held = value.reshape((-1, value.shape[-1]))
        self.round = 0
        self.start()

    @property
    def rounds(self):
        return 2 * self.bits

    def stage(self):
        return min(self.round, self.rounds - 1 - self.round)

    def mine(self):
        stage = self.stage()
        bit = jnp.where(self.core % 2 == 0, self.orders[0][stage], self.orders[1][stage])
        return (self.place >> bit) & 1

    def start(self):
        stage, mine = self.stage(), self.mine()
        if self.round < self.bits:
            halves = self.held.reshape((2, -1, self.shape[-1]))
            self.sent = lax.dynamic_index_in_dim(halves, 1 - mine, 0, keepdims=False)
            self.kept = lax.dynamic_index_in_dim(halves, mine, 0, keepdims=False)
        else:
            self.sent = self.kept = self.held
        pairs = [
            (a * self.cores + c, (a ^ (1 << self.orders[c % 2][stage])) * self.cores + c)
            for a in range(self.count)
            for c in range(self.cores)
        ]
        self.arriving = lax.ppermute(self.sent, ("asset", "sample"), pairs)

    def step(self):
        if self.round < self.bits:
            self.held = self.kept + self.arriving
        else:
            self.held = jnp.where(
                self.mine() == 0,
                jnp.concatenate([self.kept, self.arriving], axis=0),
                jnp.concatenate([self.arriving, self.kept], axis=0),
            )
        self.round += 1
        if self.round < self.rounds:
            self.start()

    def finish(self):
        while self.round < self.rounds:
            self.step()
        return self.held.reshape(self.shape)


def total_small(value):
    count, cores = lax.axis_size("asset"), lax.axis_size("sample")
    bits = count.bit_length() - 1
    orders = [list(range(bits)), list(range(1, bits)) + [0]]
    for stage in range(bits):
        pairs = [
            (a * cores + c, (a ^ (1 << orders[c % 2][stage])) * cores + c)
            for a in range(count)
            for c in range(cores)
        ]
        value = value + lax.ppermute(value, ("asset", "sample"), pairs)
    return value


def shards(samples, start_panel):
    rows, size = start_panel.shape
    width_all = rows * lax.axis_size("asset")
    core = lax.axis_index("sample")
    swap = lambda held: lax.ppermute(held, "sample", [(0, 1), (1, 0)])
    steps = rows // min(WIDTH, rows)
    slices = next(n for n in (4, 2, 1) if steps % n == 0)
    few = min(2, slices)
    none = jnp.zeros((8, 128), jnp.float32)
    added = lambda values: functools.reduce(jnp.add, values)

    def beside(run, total):
        result = run(total.sent)
        if total.round < total.rounds:
            result, total.arriving = lax.optimization_barrier((result, total.arriving))
            total.step()
        return result

    def step_both(leading, trailing, rounds):
        while leading.round < leading.rounds:
            leading.step()
            if trailing.round < rounds:
                trailing.step()

    first0 = Total(project(samples, 0, start_panel, 1, 0, none))
    parts = [
        beside(lambda token: project(samples, 1, start_panel, few, k, token), first0)
        for k in range(few)
    ]
    first1 = Total(added(parts))
    step_both(first0, first1, first1.rounds - slices)
    scores0 = first0.finish()
    parts = [
        beside(lambda token: apply(samples, 0, scores0, slices, k, token), first1)
        for k in range(slices)
    ]
    second0 = Total(added(parts))
    scores1 = first1.finish()
    parts = [
        beside(lambda token: apply(samples, 1, scores1, slices, k, token), second0)
        for k in range(slices)
    ]
    second1 = Total(added(parts))
    step_both(second0, second1, 2)
    following0 = second0.finish()
    normal0 = beside(lambda token: normalise(scores0, following0, width_all, token), second1)
    own0 = None
    for k in range(few):
        own0 = beside(
            lambda token: expand(samples, 0, normal0, few, k, token, own0), second1
        )
    other0 = swap(own0)
    normal1 = normalise(scores1, second1.finish(), width_all, none)
    own1 = expand(samples, 1, normal1, 1, 0, none)
    other1 = swap(own1)
    starts = jnp.einsum(
        "gks,gls->gkl",
        jnp.stack([normal0, normal1]),
        jnp.stack([scores0, scores1]),
        precision=HIGH,
    )
    other_starts = swap(starts)
    own_grams = partial_grams(own_gram_kernel, 3, (own0, own1), [])
    wide = pltpu.VMEM((2 * size, 2 * size), jnp.float32)
    cross_grams = partial_grams(cross_gram_kernel, 2, (own0, own1, other0, other1), [wide])
    grams = total_small(jnp.concatenate([own_grams, cross_grams]))
    other_grams = swap(grams)
    ordered = lambda a, b: (jnp.where(core == 0, a, b), jnp.where(core == 0, b, a))
    inverses, weights = final_iterations(
        *ordered(grams, other_grams), *ordered(starts, other_starts), width_all
    )
    return outputs((own0, own1), (other0, other1), inverses, weights)


def solution(mesh):
    placed = (P(("rep", "sample"), None, "asset"), P("asset", None))
    return jax.shard_map(
        shards,
        mesh=mesh,
        in_specs=placed,
        out_specs=(P(("rep", "sample"), "asset", None), P(("rep", "asset"), None)),
        check_vma=False,
    )
```

```python
import functools

import jax
import jax.numpy as jnp
from jax import lax
from jax.experimental import pallas as pl
from jax.experimental.pallas import tpu as pltpu
from jax.sharding import PartitionSpec as P

LOCAL_ITERS = 2
FINAL_ITERS = 4


HIGH = lax.Precision.HIGHEST
TILE = 8
PANEL = 4
WIDTH = 512
PART = 256
ROWS = 1024
MEGA = 1024 * 1024


def dot_exact(left, right, dims):
    return lax.dot_general(
        left, right, (dims, ((), ())), precision=HIGH, preferred_element_type=jnp.float32
    )


def inverse_factors(matrices):
    size = matrices[0].shape[0]
    blocks = size // TILE
    full = (TILE, size)
    sublane = lax.broadcasted_iota(jnp.int32, full, 0)
    lane = lax.broadcasted_iota(jnp.int32, full, 1)
    left, right, scales = [], [], []
    for matrix in matrices:
        symmetric = 0.5 * (matrix + matrix.T)
        rows = [symmetric[TILE * i : TILE * (i + 1)] for i in range(blocks)]
        on_diagonal = [
            jnp.where(lane == sublane + TILE * i, row, 0.0) for i, row in enumerate(rows)
        ]
        along_lanes = lax.rsqrt(jnp.sum(sum(on_diagonal), axis=0, keepdims=True))
        scales.append(jnp.broadcast_to(along_lanes, full))
        left.append(
            [
                row
                * lax.rsqrt(jnp.broadcast_to(jnp.sum(own, axis=1, keepdims=True), full))
                * scales[-1]
                for row, own in zip(rows, on_diagonal)
            ]
        )
        right.append(
            [jnp.where(lane == sublane + TILE * i, 1.0, 0.0) for i in range(blocks)]
        )
    along = lambda block, row: jnp.broadcast_to(block[row : row + 1], full)
    across = lambda block, column: jnp.broadcast_to(block[:, column : column + 1], full)
    for panel in range(0, blocks, PANEL):
        last = panel + PANEL
        for j in range(panel, last):
            for a, b in zip(left, right):
                columns = [across(a[j], TILE * j + k) for k in range(TILE)]
                d = [[along(columns[k], i) for k in range(i + 1)] for i in range(TILE)]
                scale = []
                for k in range(0, TILE, 2):
                    corner, side, end = d[k][k], d[k + 1][k], d[k + 1][k + 1]
                    determinant = corner * end - side * side
                    scale.append(lax.rsqrt(corner))
                    scale.append(lax.rsqrt(determinant) * (corner * scale[k]))
                    d[k + 1][k] = side * scale[k]
                    for i in range(k + 2, TILE):
                        d[i][k] = d[i][k] * scale[k]
                        d[i][k + 1] = (d[i][k + 1] - d[i][k] * d[k + 1][k]) * scale[k + 1]
                    for i in range(k + 2, TILE):
                        for m in range(k + 2, i + 1):
                            d[i][m] = d[i][m] - (
                                d[i][k] * d[m][k] + d[i][k + 1] * d[m][k + 1]
                            )

                def substitute(parts):
                    for k in range(TILE):
                        for m in range(k):
                            parts[k] = parts[k] - d[k][m] * parts[m]
                        parts[k] = parts[k] * scale[k]
                    return parts

                rows_a = substitute([along(a[j], k) for k in range(TILE)])
                rows_b = substitute([along(b[j], k) for k in range(TILE)])
                for i in range(j + 1, last):
                    weights = substitute([across(a[i], TILE * j + k) for k in range(TILE)])
                    for k in range(TILE):
                        a[i] = a[i] - weights[k] * rows_a[k]
                        b[i] = b[i] - weights[k] * rows_b[k]

                def gather(rows):
                    block = rows[0]
                    for k in range(1, TILE):
                        block = jnp.where(sublane == k, rows[k], block)
                    return block

                a[j], b[j] = gather(rows_a), gather(rows_b)
        if last < blocks:
            for a, b in zip(left, right):
                top_a = jnp.concatenate(a[panel:last], axis=0)
                top_b = jnp.concatenate(b[panel:last], axis=0)
                change = dot_exact(
                    top_a[:, TILE * last :],
                    jnp.concatenate([top_a, top_b], axis=1),
                    ((0,), (0,)),
                )
                for i in range(last, blocks):
                    rows = change[TILE * (i - last) : TILE * (i - last + 1)]
                    a[i] = a[i] - rows[:, :size]
                    b[i] = b[i] - rows[:, size:]
    return [
        jnp.concatenate([row * scale for row in b], axis=0) for b, scale in zip(right, scales)
    ]


def split(value):
    high = value.astype(jnp.bfloat16)
    return high, (value - high.astype(jnp.float32)).astype(jnp.bfloat16)


def dot_short(left, right, dims=((1,), (0,))):
    return lax.dot_general(left, right, (dims, ((), ())), preferred_element_type=jnp.float32)


def call(body, grid, in_specs, out_specs, out_shape, scratch, flops, read, aliases={}, limit=52):
    return pl.pallas_call(
        body,
        grid=grid,
        in_specs=in_specs,
        out_specs=out_specs,
        out_shape=out_shape,
        scratch_shapes=scratch,
        input_output_aliases=aliases,
        compiler_params=pltpu.CompilerParams(vmem_limit_bytes=limit * MEGA),
        cost_estimate=pl.CostEstimate(flops=flops, bytes_accessed=read, transcendentals=0),
    )


TOKEN = pl.BlockSpec(memory_space=pl.ANY)


def project_kernel(x_ref, panel_ref, token_ref, out_ref, total):
    step = pl.program_id(0)
    size = panel_ref.shape[1]

    @pl.when(step == 0)
    def _():
        total[...] = jnp.zeros_like(total)

    high, low = split(x_ref[0])
    panel_high, panel_low = split(panel_ref[...])
    sides = jnp.concatenate(
        [
            jnp.concatenate([panel_high, panel_low], axis=1),
            jnp.concatenate([panel_high, jnp.zeros_like(panel_low)], axis=1),
        ],
        axis=0,
    )
    total[...] += dot_short(jnp.concatenate([high, low], axis=1), sides)

    @pl.when(step == pl.num_programs(0) - 1)
    def _():
        out_ref[...] = (total[:, :size] + total[:, size:]).T


def project(samples, group, panel, slices, index, token):
    _, length, rows = samples.shape
    size = panel.shape[1]
    width = min(WIDTH, rows)
    steps = rows // width // slices
    first = steps * index
    return call(
        project_kernel,
        (steps,),
        [
            pl.BlockSpec((1, length, width), lambda i: (group, 0, first + i)),
            pl.BlockSpec((width, size), lambda i: (first + i, 0)),
            TOKEN,
        ],
        pl.BlockSpec((size, length), lambda i: (0, 0)),
        jax.ShapeDtypeStruct((size, length), jnp.float32),
        [pltpu.VMEM((length, 2 * size), jnp.float32)],
        8 * length * steps * width * size,
        4 * length * steps * width,
    )(samples, panel, token)


def expand_part(pair, high, low):
    size = pair.shape[0] // 2
    both = dot_short(pair, high)
    return (both[:size] + both[size:]) + dot_short(pair[:size], low)


def apply_kernel(x_ref, scores_ref, token_ref, out_ref, pair, total):
    step = pl.program_id(0)
    size = scores_ref.shape[0]

    @pl.when(step == 0)
    def _():
        pair[...] = jnp.concatenate(split(scores_ref[...]), axis=0)
        total[...] = jnp.zeros_like(total)

    width = x_ref.shape[2]
    part = min(PART, width)
    halves = [split(x_ref[0, :, at : at + part]) for at in range(0, width, part)]
    expanded = [split(expand_part(pair[...], high, low)) for high, low in halves]
    tops = [top for top, _ in expanded]
    rests = [rest for _, rest in expanded]
    sides = jnp.concatenate(
        [
            jnp.concatenate(tops + tops, axis=1),
            jnp.concatenate(rests + [jnp.zeros_like(rest) for rest in rests], axis=1),
        ],
        axis=0,
    )
    left = jnp.concatenate([high for high, _ in halves] + [low for _, low in halves], axis=1)
    total[...] += dot_short(left, sides, ((1,), (1,)))

    @pl.when(step == pl.num_programs(0) - 1)
    def _():
        out_ref[...] = total[:, :size] + total[:, size:]


def apply(samples, group, scores, slices, index, token):
    _, length, rows = samples.shape
    size = scores.shape[0]
    width = min(WIDTH, rows)
    steps = rows // width // slices
    first = steps * index
    return call(
        apply_kernel,
        (steps,),
        [
            pl.BlockSpec((1, length, width), lambda i: (group, 0, first + i)),
            pl.BlockSpec((size, length), lambda i: (0, 0)),
            TOKEN,
        ],
        pl.BlockSpec((length, size), lambda i: (0, 0)),
        jax.ShapeDtypeStruct((length, size), jnp.float32),
        [
            pltpu.VMEM((2 * size, length), jnp.bfloat16),
            pltpu.VMEM((length, 2 * size), jnp.float32),
        ],
        16 * length * steps * width * size,
        4 * length * steps * width,
    )(samples, scores, token)


def expand_kernel(x_ref, scores_ref, token_ref, *rest):
    out_ref, pair = rest[-2:]

    @pl.when(pl.program_id(0) == 0)
    def _():
        pair[...] = jnp.concatenate(split(scores_ref[...]), axis=0)

    width = x_ref.shape[2]
    part = min(PART, width)
    for at in range(0, width, part):
        high, low = split(x_ref[0, :, at : at + part])
        out_ref[at : at + part] = expand_part(pair[...], high, low).T


def expand(samples, group, scores, slices, index, token, before=None):
    _, length, rows = samples.shape
    size = scores.shape[0]
    width = min(WIDTH, rows)
    steps = rows // width // slices
    first = steps * index
    earlier = [] if before is None else [before]
    return call(
        expand_kernel,
        (steps,),
        [
            pl.BlockSpec((1, length, width), lambda i: (group, 0, first + i)),
            pl.BlockSpec((size, length), lambda i: (0, 0)),
            TOKEN,
            *[TOKEN for _ in earlier],
        ],
        pl.BlockSpec((width, size), lambda i: (first + i, 0)),
        jax.ShapeDtypeStruct((rows, size), jnp.float32),
        [pltpu.VMEM((2 * size, length), jnp.bfloat16)],
        8 * length * steps * width * size,
        4 * length * steps * width,
        {3: 0} if earlier else {},
    )(samples, scores, token, *earlier)


def normal_kernel(width_all, first_ref, second_ref, token_ref, out_ref):
    gram = dot_exact(first_ref[...], second_ref[...], ((1,), (0,))) * (1.0 / width_all)
    (inverse,) = inverse_factors([gram])
    out_ref[...] = dot_exact(inverse, second_ref[...], ((1,), (1,)))


def normalise(first, second, width_all, token):
    size, length = first.shape
    whole = lambda held: pl.BlockSpec(held.shape, lambda: (0, 0))
    return pl.pallas_call(
        functools.partial(normal_kernel, width_all),
        in_specs=[whole(first), whole(second), TOKEN],
        out_specs=whole(first),
        out_shape=jax.ShapeDtypeStruct((size, length), jnp.float32),
        compiler_params=pltpu.CompilerParams(vmem_limit_bytes=40 * MEGA),
        cost_estimate=pl.CostEstimate(
            flops=6_000_000_000, bytes_accessed=4 * 3 * size * length, transcendentals=0
        ),
    )(first, second, token)


def own_gram_kernel(own0, own1, out_ref):
    @pl.when(pl.program_id(0) == 0)
    def _():
        out_ref[...] = jnp.zeros_like(out_ref)

    size = own0.shape[1]
    first = ((0,), (0,))
    high, low = split(jnp.concatenate([own0[...], own1[...]], axis=1))
    both = dot_short(high, jnp.concatenate([high, low], axis=1), first)
    mixed = both[:, 2 * size :]
    gram = both[:, : 2 * size] + (dot_short(low, low, first) + (mixed + mixed.T))
    out_ref[0] += gram[:size, :size]
    out_ref[1] += gram[:size, size:]
    out_ref[2] += gram[size:, size:]


def cross_gram_kernel(own0, own1, other0, other1, out_ref, total):
    step = pl.program_id(0)

    @pl.when(step == 0)
    def _():
        total[...] = jnp.zeros_like(total)

    size = own0.shape[1]
    first = ((0,), (0,))
    high, low = split(jnp.concatenate([own0[...], own1[...]], axis=1))
    right, rest = split(jnp.concatenate([other0[...], other1[...]], axis=1))
    both = dot_short(high, jnp.concatenate([right, rest], axis=1), first)
    total[...] += both[:, : 2 * size] + (both[:, 2 * size :] + dot_short(low, right, first))

    @pl.when(step == pl.num_programs(0) - 1)
    def _():
        swapped = lax.rem(lax.axis_index("sample"), 2) == 1
        pick = lambda rows, a, b: jnp.where(swapped, total[rows, b], total[rows, a])
        front, back = slice(0, size), slice(size, 2 * size)
        out_ref[0] = pick(front, front, back)
        out_ref[1] = pick(back, back, front)


def partial_grams(body, count, panels, scratch):
    rows, size = panels[0].shape
    height = min(ROWS, rows)
    return call(
        body,
        (rows // height,),
        [pl.BlockSpec((height, size), lambda i: (i, 0))] * len(panels),
        pl.BlockSpec((count, size, size), lambda i: (0, 0, 0)),
        jax.ShapeDtypeStruct((count, size, size), jnp.float32),
        scratch,
        2 * 30 * rows * size * size,
        4 * len(panels) * rows * size,
        limit=60,
    )(*panels)


def final_kernel(
    width_all, first, second, start0, start1, inverse_ref, out_ref, gram, matrix, held, product
):
    count, size, _ = inverse_ref.shape
    at = lambda g: slice(g * size, (g + 1) * size)
    places = (
        (first, ((0, 0), (0, 1), (1, 1), (0, 2), (1, 3))),
        (second, ((2, 2), (2, 3), (3, 3), (2, 1), (3, 0))),
    )
    for parts, where in places:
        for k, (g, h) in enumerate(where):
            gram[at(g), at(h)] = parts[k]
            if g != h:
                gram[at(h), at(g)] = parts[k].T
    inverses = inverse_factors(
        [gram[at(g), at(g)] * (1.0 / width_all) for g in range(count)]
    )
    starts = [start0[0], start0[1], start1[0], start1[1]]
    for g in range(count):
        inverse_ref[g] = inverses[g]
        held[at(g), :] = dot_exact(inverses[g] * (1.0 / count), starts[g], ((1,), (0,)))
        gram[at(g), :] = dot_exact(inverses[g], gram[at(g), :], ((1,), (0,)))
    for h in range(count):
        matrix[:, at(h)] = dot_exact(gram[:, at(h)], inverses[h], ((1,), (1,)))
    product[...] = dot_exact(matrix[...], held[...], ((1,), (0,)))

    def step(_, carry):
        small = dot_exact(held[...], product[...], ((0,), (0,))) * (1.0 / width_all)
        following = product[...] * (1.0 / count)
        ahead = dot_exact(matrix[...], following, ((1,), (0,)))
        (inverse,) = inverse_factors([small])
        weights = dot_exact(held[...], inverse, ((1,), (1,)))
        for g in range(count):
            out_ref[g] = weights[at(g)]
        held[...] = dot_exact(following, inverse, ((1,), (1,)))
        product[...] = dot_exact(ahead, inverse, ((1,), (1,)))
        return carry

    lax.fori_loop(0, FINAL_ITERS, step, 0)
    for g in range(count):
        out_ref[g] = dot_exact(inverse_ref[g], out_ref[g], ((0,), (0,)))


def final_iterations(first, second, start0, start1, width_all):
    size = first.shape[-1]
    groups_all = 4
    out = jax.ShapeDtypeStruct((groups_all, size, size), jnp.float32)
    wide = groups_all * size
    return pl.pallas_call(
        functools.partial(final_kernel, width_all),
        out_shape=(out, out),
        scratch_shapes=[
            pltpu.VMEM((wide, wide), jnp.float32),
            pltpu.VMEM((wide, wide), jnp.float32),
            pltpu.VMEM((wide, size), jnp.float32),
            pltpu.VMEM((wide, size), jnp.float32),
        ],
        compiler_params=pltpu.CompilerParams(vmem_limit_bytes=40 * MEGA),
    )(first, second, start0, start1)


def output_kernel(own0, own1, other0, other1, inverse_ref, weight_ref, panel_ref, out_ref, sides):
    size = own0.shape[1]
    core = lax.rem(lax.axis_index("sample"), 2)

    @pl.when(pl.program_id(0) == 0)
    def _():
        def side(value, slot):
            high, low = split(value)
            sides[slot, :size, :size] = high
            sides[slot, :size, size:] = low
            sides[slot, size:, :size] = high
            sides[slot, size:, size:] = jnp.zeros_like(low)

        for g in range(2):
            side(inverse_ref[2 * core + g].T, g)
            side(weight_ref[2 * core + g], 2 + g)
            side(weight_ref[2 * (1 - core) + g], 4 + g)

    def product(halves, slot):
        both = dot_short(halves, sides[slot])
        return both[:, :size] + both[:, size:]

    sums = []
    for k, pair in enumerate(((own0, own1), (other0, other1))):
        parts = []
        for g in range(2):
            halves = jnp.concatenate(split(pair[g][...]), axis=1)
            if k == 0:
                panel_ref[g] = product(halves, g)
            parts.append(product(halves, 2 * (k + 1) + g))
        sums.append(parts[0] + parts[1])
    out_ref[...] = sums[0] + sums[1]


def outputs(own, other, inverses, weights):
    rows, size = own[0].shape
    height = min(ROWS // 2, rows)
    whole = pl.BlockSpec(inverses.shape, lambda i: (0, 0, 0))
    return call(
        output_kernel,
        (rows // height,),
        [pl.BlockSpec((height, size), lambda i: (i, 0))] * 4 + [whole, whole],
        (
            pl.BlockSpec((2, height, size), lambda i: (0, i, 0)),
            pl.BlockSpec((height, size), lambda i: (i, 0)),
        ),
        (
            jax.ShapeDtypeStruct((2, rows, size), jnp.float32),
            jax.ShapeDtypeStruct((rows, size), jnp.float32),
        ),
        [pltpu.VMEM((6, 2 * size, 2 * size), jnp.bfloat16)],
        2 * 24 * rows * size * size,
        4 * 7 * rows * size,
    )(*own, *other, inverses, weights)


class Total:
    def __init__(self, value):
        self.count, self.cores = lax.axis_size("asset"), lax.axis_size("sample")
        self.bits = self.count.bit_length() - 1
        self.orders = [list(range(self.bits)), list(range(1, self.bits)) + [0]]
        self.place, self.core = lax.axis_index("asset"), lax.axis_index("sample")
        self.shape = value.shape
        self.held = value.reshape((-1, value.shape[-1]))
        self.round = 0
        self.start()

    @property
    def rounds(self):
        return 2 * self.bits

    def stage(self):
        return min(self.round, self.rounds - 1 - self.round)

    def mine(self):
        stage = self.stage()
        bit = jnp.where(self.core % 2 == 0, self.orders[0][stage], self.orders[1][stage])
        return (self.place >> bit) & 1

    def start(self):
        stage, mine = self.stage(), self.mine()
        if self.round < self.bits:
            halves = self.held.reshape((2, -1, self.shape[-1]))
            self.sent = lax.dynamic_index_in_dim(halves, 1 - mine, 0, keepdims=False)
            self.kept = lax.dynamic_index_in_dim(halves, mine, 0, keepdims=False)
        else:
            self.sent = self.kept = self.held
        pairs = [
            (a * self.cores + c, (a ^ (1 << self.orders[c % 2][stage])) * self.cores + c)
            for a in range(self.count)
            for c in range(self.cores)
        ]
        self.arriving = lax.ppermute(self.sent, ("asset", "sample"), pairs)

    def step(self):
        if self.round < self.bits:
            self.held = self.kept + self.arriving
        else:
            self.held = jnp.where(
                self.mine() == 0,
                jnp.concatenate([self.kept, self.arriving], axis=0),
                jnp.concatenate([self.arriving, self.kept], axis=0),
            )
        self.round += 1
        if self.round < self.rounds:
            self.start()

    def finish(self):
        while self.round < self.rounds:
            self.step()
        return self.held.reshape(self.shape)


class SmallTotal:
    def __init__(self, value):
        self.count, self.cores = lax.axis_size("asset"), lax.axis_size("sample")
        self.rounds = self.count.bit_length() - 1
        bits = list(range(self.rounds))
        self.orders = [bits, bits[1:] + bits[:1]]
        self.held, self.round = value, 0
        self.start()

    def start(self):
        pairs = [
            (a * self.cores + c, (a ^ (1 << self.orders[c % 2][self.round])) * self.cores + c)
            for a in range(self.count)
            for c in range(self.cores)
        ]
        self.sent = self.held
        self.arriving = lax.ppermute(self.sent, ("asset", "sample"), pairs)

    def step(self):
        self.held = self.held + self.arriving
        self.round += 1
        if self.round < self.rounds:
            self.start()


def shards(samples, start_panel):
    rows, size = start_panel.shape
    width_all = rows * lax.axis_size("asset")
    core = lax.axis_index("sample")
    swap = lambda held: lax.ppermute(held, "sample", [(0, 1), (1, 0)])
    steps = rows // min(WIDTH, rows)
    slices = next(n for n in (4, 2, 1) if steps % n == 0)
    few = min(2, slices)
    none = jnp.zeros((8, 128), jnp.float32)
    added = lambda values: functools.reduce(jnp.add, values)

    def beside(run, total):
        result = run(total.sent)
        if total.round < total.rounds:
            result, total.arriving = lax.optimization_barrier((result, total.arriving))
            total.step()
        return result

    def step_both(leading, trailing, rounds):
        while leading.round < leading.rounds:
            leading.step()
            if trailing.round < rounds:
                trailing.step()

    first0 = Total(project(samples, 0, start_panel, 1, 0, none))
    parts = [
        beside(lambda token: project(samples, 1, start_panel, slices, k, token), first0)
        for k in range(slices)
    ]
    first1 = Total(added(parts))
    step_both(first0, first1, first1.rounds - slices)
    scores0 = first0.finish()
    parts = [
        beside(lambda token: apply(samples, 0, scores0, slices, k, token), first1)
        for k in range(slices)
    ]
    second0 = Total(added(parts))
    scores1 = first1.finish()
    parts = [
        beside(lambda token: apply(samples, 1, scores1, slices, k, token), second0)
        for k in range(slices)
    ]
    second1 = Total(added(parts))
    step_both(second0, second1, 2)
    following0 = second0.finish()
    normal0 = beside(lambda token: normalise(scores0, following0, width_all, token), second1)
    own0 = None
    for k in range(few):
        own0 = beside(
            lambda token: expand(samples, 0, normal0, few, k, token, own0), second1
        )
    other0 = swap(own0)
    normal1 = normalise(scores1, second1.finish(), width_all, none)
    own1 = expand(samples, 1, normal1, 1, 0, none)
    other1 = swap(own1)
    starts = jnp.einsum(
        "gks,gls->gkl",
        jnp.stack([normal0, normal1]),
        jnp.stack([scores0, scores1]),
        precision=HIGH,
    )
    other_starts = swap(starts)
    own_grams = partial_grams(own_gram_kernel, 3, (own0, own1), [])
    wide = pltpu.VMEM((2 * size, 2 * size), jnp.float32)
    own_total = SmallTotal(own_grams)
    cross_total = SmallTotal(
        beside(
            lambda token: partial_grams(
                cross_gram_kernel, 2, (own0, own1, other0, other1), [wide]
            ),
            own_total,
        )
    )
    while cross_total.round < cross_total.rounds:
        if own_total.round < own_total.rounds:
            own_total.step()
        cross_total.step()
    grams = jnp.concatenate([own_total.held, cross_total.held])
    other_grams = swap(grams)
    ordered = lambda a, b: (jnp.where(core == 0, a, b), jnp.where(core == 0, b, a))
    inverses, weights = final_iterations(
        *ordered(grams, other_grams), *ordered(starts, other_starts), width_all
    )
    return outputs((own0, own1), (other0, other1), inverses, weights)


def solution(mesh):
    placed = (P(("rep", "sample"), None, "asset"), P("asset", None))
    return jax.shard_map(
        shards,
        mesh=mesh,
        in_specs=placed,
        out_specs=(P(("rep", "sample"), "asset", None), P(("rep", "asset"), None)),
        check_vma=False,
    )
```
